1024 devices in a mesh: dp: 256 (over x, z, core), tensor: 4 (over y).
Axes of the slice: x: 4, y: 4, z: 32, core: 2. Of those that a mesh axis runs over, the one named last changes fastest.
Arguments:
- out_grad: bfloat16 [49152, 4096], P('dp'), may hold values from -24 to 24
- saved_input: bfloat16 [49152, 2048], P('dp', 'tensor'), may hold values from -6 to 6
- weight: bfloat16 [2048, 4096], P('tensor'), may hold values from -0.09375 to 0.09375
- amax_history: float32 [16], replicated, may hold values from 100 to 250
Outputs:
- input_grad: bfloat16 [49152, 2048], P('dp', 'tensor')
- weight_grad_q: bfloat16 [2048, 4096], P('tensor', 'dp')
- new_history: float32 [16], replicated
The draws below stay inside these ranges and needn't reach their ends.
All inputs are finite; a program needn't handle non-finite values.
Results may differ from the reference program's by a relative error of at most 0.0051.
Values sent between devices are 32-bit elements; how exact they have to be, the bound alone decides.
A program may use at most 32 MiB of HBM per device.

```python
import math
import jax
import jax.numpy as jnp
from jax import lax

DIN_DEV = 512
DOUT = 4096
HIST = 16
TOK_DEV = 192
DIN = 2048
TOKENS = 49152
N_DP = 256
N_TENSOR = 4


def block_boost(rows, columns, blocks):
    token_block = jnp.arange(rows, dtype=jnp.int32) // (rows // blocks)
    column_block = jnp.arange(columns, dtype=jnp.int32) // (columns // blocks)
    offset = (column_block[None, :] - token_block[:, None]) % blocks
    return jnp.where((offset == 0) | (offset == blocks // 2), 6.0, 1.0).astype(jnp.float32)


def draw_out_grad(key, part):
    key = jax.random.fold_in(key, 11)
    rows = N_DP * TOK_DEV
    base = jnp.clip(jax.random.normal(key, (rows, DOUT), jnp.float32), -4.0, 4.0)
    return (base * block_boost(rows, DOUT, N_DP)).astype(jnp.bfloat16)


def levels(stream_key, dims, cuts, low, largest):
    def one(axis_at, shards_of):
        heights = jax.random.uniform(jax.random.fold_in(jax.random.fold_in(stream_key, 6), axis_at), (shards_of,), jnp.float32, low / len(cuts), largest / len(cuts))
        return jnp.repeat(jnp.exp(heights), dims[axis_at] // shards_of).reshape((-1,) + (1,) * (len(dims) - axis_at - 1))

    factor_of = one(*cuts[0])
    for cut in cuts[1:]:
        factor_of = factor_of * one(*cut)
    return factor_of


def noise(rng, extent, scale, limit, cuts=(), kind=jnp.bfloat16):
    entries = scale * jax.random.normal(rng, extent, jnp.float32)
    if cuts:
        entries = entries * levels(rng, extent, cuts, -0.22, 0.18)
    return jnp.clip(entries, -limit, limit).astype(kind)


def setup_inputs(seed: int = 0) -> dict:
    arg_keys = jax.random.split(jax.random.key(seed), 5)
    out_grad = draw_out_grad(jax.random.fold_in(arg_keys[4], 71), 0)
    saved_input = noise(arg_keys[1], (TOKENS, DIN), 1.0, 6.0, ((0, 256), (1, 4)))
    weight = noise(arg_keys[2], (DIN, DOUT), DOUT ** -0.5, 0.09375, ((0, 4),))
    amax_history = jnp.clip(jnp.exp(jax.random.uniform(arg_keys[3], (HIST,), jnp.float32, math.log(100.0), math.log(250.0))), 100.0, 250.0)
    return {"out_grad": out_grad, "saved_input": saved_input, "weight": weight, "amax_history": amax_history}


LIMIT = 8.0


def reference(out_grad, saved_input, weight, amax_history):
    input_grad = jnp.dot(out_grad, weight.T, preferred_element_type=jnp.float32).astype(jnp.bfloat16)
    scale_in = LIMIT / jnp.max(amax_history)
    width_in = DIN_DEV * N_TENSOR
    inputs_blocks = saved_input.reshape(N_DP, TOK_DEV, width_in)
    grads_blocks = out_grad.reshape(N_DP, TOK_DEV, DOUT)

    def accumulate(running, blocks):
        term = jnp.dot(blocks[0].T, blocks[1], preferred_element_type=jnp.float32)
        quant = jnp.clip(term * scale_in, -LIMIT, LIMIT).astype(jnp.bfloat16)
        return running + quant.astype(jnp.float32), None

    summed, unused = lax.scan(accumulate, jnp.zeros((width_in, DOUT), jnp.float32), (inputs_blocks, grads_blocks))
    weight_sum = summed / scale_in
    amax = jnp.max(jnp.abs(weight_sum))
    new_history = jnp.concatenate([amax[None], amax_history[:-1]])
    out_scale = LIMIT / jnp.max(new_history)
    weight_grad_q = (weight_sum * out_scale).astype(jnp.bfloat16)
    return input_grad, weight_grad_q, new_history
```

```python
import functools

import jax
import jax.numpy as jnp
from jax import lax
from jax.experimental import pallas as pl
from jax.experimental.pallas import tpu as pltpu
from jax.sharding import PartitionSpec as P

LIMIT = 8.0
MESH = pl.DeviceIdType.MESH
NX, NZ, NY = 4, 32, 4
NB = NZ // 4
F32 = jnp.float32


def kernel(
    og_hbm, si_hbm, w_hbm, hist_ref,
    ig_out, wq_out, hist_out,
    og, si, w, ig, terms, from_core, pass_one, in_one, pass_two, in_two,
    ready, in_last, peaks_core, peaks_plane, peaks_z, peaks_end, peak,
    local_sem, send_sem, recv_sem,
):
    dp, y = lax.axis_index("dp"), lax.axis_index("tensor")
    x, z, c = dp // (2 * NZ), lax.rem(dp // 2, NZ), lax.rem(dp, 2)
    zc = lax.rem(z, 4)

    def device(x, y, z, c):
        return ((x * NZ + z) * 2 + c, y)

    def along_x(d):
        return device(lax.rem(x + d + NX, NX), y, z, c)

    def along_z(d):
        return device(x, y, lax.rem(z + d + NZ, NZ), c)

    def in_plane(dx, dy):
        return device(lax.rem(x + dx, NX), lax.rem(y + dy, NY), z, c)

    other_core = device(x, y, z, 1 - c)

    barrier = pltpu.get_barrier_semaphore()

    def greet(to):
        pl.semaphore_signal(barrier, inc=1, device_id=to, device_id_type=MESH)

    @pl.loop(1, NZ)
    def _(d):
        greet(along_z(d))

    @pl.loop(1, NX * NY)
    def _(d):
        greet(in_plane(d // NY, lax.rem(d, NY)))

    greet(other_core)

    get_og = pltpu.make_async_copy(og_hbm, og, local_sem.at[0])
    get_si = pltpu.make_async_copy(si_hbm, si, local_sem.at[1])
    get_w = pltpu.make_async_copy(w_hbm, w, local_sem.at[2])
    get_si.start()
    get_og.start()
    get_w.start()

    used = [0]
    sent = []

    def send(src, dst, to):
        n = used[0]
        used[0] += 1
        copy = pltpu.make_async_remote_copy(
            src_ref=src, dst_ref=dst, send_sem=send_sem.at[n], recv_sem=recv_sem.at[n],
            device_id=to, device_id_type=MESH,
        )
        copy.start()
        sent.append(copy)
        return copy

    scale_in = LIMIT / jnp.max(hist_ref[...])
    get_si.wait()
    get_og.wait()

    def tile(at):
        @pl.loop(0, 4)
        def _(s):
            columns = pl.ds(pl.multiple_of(at * 1024 + s * 256, 256), 256)
            term = lax.dot_general(
                og[:, columns], si[...], (((0,), (0,)), ((), ())), preferred_element_type=F32
            )
            quant = jnp.clip(term * scale_in, -LIMIT, LIMIT).astype(jnp.bfloat16).astype(F32)
            for b in range(2):
                for j in range(4):
                    for core in range(2):
                        row = b * 128 + j * 32 + core * 16
                        terms[0, core, at, j, s * 2 + b] = quant[row : row + 8]
                        terms[1, core, j, at, s * 2 + b] = quant[row + 8 : row + 16]

    first, second = (x, zc), (zc, x)

    def classes(k):
        return [lax.rem(m + k, 4) for m in first]

    core_copies = [{}, {}]

    def to_core(p, k):
        m = classes(k)[p]
        core_copies[p][k] = send(terms.at[p, 1 - c, m], from_core.at[p, m], other_core)

    def add_core(p, k):
        core_copies[p][k].wait_recv()
        m = classes(k)[p]

        @pl.loop(0, 4)
        def _(i):
            terms[p, c, m, i] += from_core[p, m, i]

    order = (2, 1, 3, 0)
    for n, k in enumerate(order):
        tile(lax.rem(x + k, 4))
        if n == 0:
            pl.semaphore_wait(barrier, NZ - 1 + NX * NY - 1 + 1)
        to_core(0, k)
    for k in order:
        to_core(1, k)

    A, B = pl.ds(0, 2), pl.ds(2, 2)
    plus = (along_x(1), along_z(1))
    minus = (along_x(-1), along_z(-1))

    one = [{}, {}]
    for p in range(2):
        m = classes(2)[p]
        add_core(p, 2)
        one[p]["a+"] = send(terms.at[p, c, m, A], pass_one.at[p, 0], plus[p])
        one[p]["a-"] = send(terms.at[p, c, m, B], pass_one.at[p, 1], minus[p])
    for p in range(2):
        add_core(p, 1)
        one[p]["b+"] = send(terms.at[p, c, classes(1)[p], B], in_one.at[p, 0, B], plus[p])
        add_core(p, 3)
        one[p]["b-"] = send(terms.at[p, c, classes(3)[p], A], in_one.at[p, 1, A], minus[p])
    for p in range(2):
        m = classes(1)[p]
        one[p]["a+"].wait_recv()
        terms[p, c, m, A] += pass_one[p, 0]
        one[p]["c+"] = send(terms.at[p, c, m, A], in_one.at[p, 0, A], plus[p])
        m = classes(3)[p]
        one[p]["a-"].wait_recv()
        terms[p, c, m, B] += pass_one[p, 1]
        one[p]["c-"] = send(terms.at[p, c, m, B], in_one.at[p, 1, B], minus[p])
    for p in range(2):
        add_core(p, 0)

    get_w.wait()

    @pl.loop(0, 2)
    def _(i):
        rows = pl.ds(pl.multiple_of(i * 256, 256), 256)
        ig[:, rows] = lax.dot_general(
            og[...], w[rows, :], (((1,), (1,)), ((), ())), preferred_element_type=F32
        ).astype(jnp.bfloat16)

    put_ig = pltpu.make_async_copy(ig, ig_out, local_sem.at[3])
    put_ig.start()

    C, D = pl.ds(0, NB // 2), pl.ds(NB // 2, NB // 2)
    two = [{}, {}]
    up, down = (plus[1], plus[0]), (minus[1], minus[0])
    for p in range(2):
        for key in ("b+", "b-", "c+", "c-"):
            one[p][key].wait_recv()
        m, n = first[p], second[p]

        def total(k):
            q = lax.rem(n + k, 4)
            terms[p, c, m, q] += in_one[p, 0, q] + in_one[p, 1, q]
            return terms.at[p, c, m, q]

        unit = total(2)
        two[p]["a+"] = send(unit.at[C], pass_two.at[p, 0], up[p])
        two[p]["a-"] = send(unit.at[D], pass_two.at[p, 1], down[p])
        two[p]["b+"] = send(total(1).at[D], in_two.at[p, 0, D], up[p])
        two[p]["b-"] = send(total(3).at[C], in_two.at[p, 1, C], down[p])
        total(0)
    for p in range(2):
        m, n = first[p], second[p]
        q = lax.rem(n + 1, 4)
        two[p]["a+"].wait_recv()
        terms[p, c, m, q, C] += pass_two[p, 0]
        two[p]["c+"] = send(terms.at[p, c, m, q, C], in_two.at[p, 0, C], up[p])
        q = lax.rem(n + 3, 4)
        two[p]["a-"].wait_recv()
        terms[p, c, m, q, D] += pass_two[p, 1]
        two[p]["c-"] = send(terms.at[p, c, m, q, D], in_two.at[p, 1, D], down[p])
    for p in range(2):
        for key in ("b+", "b-", "c+", "c-"):
            two[p][key].wait_recv()
        ready[:, p] = terms[p, c, first[p], second[p]] + in_two[p, 0] + in_two[p, 1]

    last = []
    mine = z // 4
    for k in sorted(range(1, NB), key=lambda k: -min(k, NB - k)):
        last.append(
            send(ready.at[lax.rem(mine + k, NB)], in_last.at[k - 1], along_z(4 * k))
        )
    for copy in last:
        copy.wait_recv()
    summed = ready[mine]
    for k in range(NB - 1):
        summed = summed + in_last[k]
    weight_sum = summed / scale_in

    def largest(values):
        return jnp.max(values, axis=(0, 1), keepdims=True)

    one_row = pl.ds(0, 1)

    def put_peak(n, value):
        peak[n] = jnp.broadcast_to(value, (8, 128))

    top = largest(jnp.max(jnp.abs(weight_sum), axis=0))
    put_peak(0, top)
    send(peak.at[0, one_row], peaks_core.at[one_row], other_core).wait_recv()
    put_peak(1, jnp.maximum(top, peaks_core[0:1, 0:1]))
    plane = [
        send(peak.at[1, one_row], peaks_plane.at[d, one_row], in_plane(d // NY, d % NY))
        for d in range(1, NX * NY)
    ]
    for copy in plane:
        copy.wait_recv()
    best = peak[1, 0:1, :]
    for d in range(1, NX * NY):
        best = jnp.maximum(best, peaks_plane[d, 0:1, :])
    put_peak(2, best)
    way = 1 - 2 * c
    ring = [
        send(peak.at[2, one_row], peaks_z.at[k - 1, one_row], along_z(way * k))
        for k in range(NZ // 2, 0, -1)
    ]
    for copy in ring:
        copy.wait_recv()
    for k in range(NZ // 2):
        best = jnp.maximum(best, peaks_z[k, 0:1, :])
    put_peak(3, best)
    send(peak.at[3, one_row], peaks_end.at[one_row], other_core).wait_recv()
    amax = jnp.maximum(best, peaks_end[0:1, :])

    history = hist_ref[...]
    lane = lax.broadcasted_iota(jnp.int32, (1, 16), 1)
    new_history = jnp.where(lane == 0, amax[:, 0:16], jnp.roll(history, 1, axis=1))
    hist_out[...] = new_history
    out_scale = LIMIT / jnp.max(new_history)
    wq_out[...] = (weight_sum * out_scale).reshape(16, 512)

    for copy in sent:
        copy.wait_send()
    put_ig.wait()


N_SENT = 8 + 12 + 12 + (NB - 1) + 1 + (NX * NY - 1) + NZ // 2 + 1


def shards(out_grad, saved_input, weight, amax_history):
    any_space = pl.BlockSpec(memory_space=pl.ANY)
    vmem = pl.BlockSpec(memory_space=pltpu.VMEM)
    input_grad, weight_q, history = pl.pallas_call(
        kernel,
        out_shape=(
            jax.ShapeDtypeStruct((192, 512), jnp.bfloat16),
            jax.ShapeDtypeStruct((16, 512), F32),
            jax.ShapeDtypeStruct((1, 16), F32),
        ),
        in_specs=[any_space, any_space, any_space, vmem],
        out_specs=[any_space, vmem, vmem],
        scratch_shapes=[
            pltpu.VMEM((192, 4096), jnp.bfloat16),
            pltpu.VMEM((192, 512), jnp.bfloat16),
            pltpu.VMEM((512, 4096), jnp.bfloat16),
            pltpu.VMEM((192, 512), jnp.bfloat16),
            pltpu.VMEM((2, 2, 4, 4, NB, 8, 512), F32),
            pltpu.VMEM((2, 4, 4, NB, 8, 512), F32),
            pltpu.VMEM((2, 2, 2, NB, 8, 512), F32),
            pltpu.VMEM((2, 2, 4, NB, 8, 512), F32),
            pltpu.VMEM((2, 2, NB // 2, 8, 512), F32),
            pltpu.VMEM((2, 2, NB, 8, 512), F32),
            pltpu.VMEM((NB, 2, 8, 512), F32),
            pltpu.VMEM((NB - 1, 2, 8, 512), F32),
            pltpu.VMEM((8, 128), F32),
            pltpu.VMEM((NX * NY, 8, 128), F32),
            pltpu.VMEM((NZ // 2, 8, 128), F32),
            pltpu.VMEM((8, 128), F32),
            pltpu.VMEM((4, 8, 128), F32),
            pltpu.SemaphoreType.DMA((4,)),
            pltpu.SemaphoreType.DMA((N_SENT,)),
            pltpu.SemaphoreType.DMA((N_SENT,)),
        ],
        compiler_params=pltpu.CompilerParams(
            collective_id=0, has_side_effects=True, vmem_limit_bytes=60 * 2**20
        ),
        name="all_steps",
    )(out_grad, saved_input, weight, amax_history.reshape(1, 16))
    return (input_grad, weight_q.T.astype(jnp.bfloat16), history.reshape(16))


def solution(mesh):
    placed = (P("dp", None), P("dp", "tensor"), P("tensor", None), P())
    return jax.shard_map(
        shards,
        mesh=mesh,
        in_specs=placed,
        out_specs=(P("dp", "tensor"), P("tensor", "dp"), P()),
        check_vma=False,
    )
```

```python
import jax
import jax.numpy as jnp
from jax import lax
from jax.experimental import pallas as pl
from jax.experimental.pallas import tpu as pltpu
from jax.sharding import PartitionSpec as P

LIMIT = 8.0
MESH = pl.DeviceIdType.MESH
NX, NZ, NY = 4, 32, 4
NB = NZ // 4
F32, BF16 = jnp.float32, jnp.bfloat16
ORDER = (2, 1, 3, 0)
PLACE = {k: n for n, k in enumerate(ORDER)}
N_SENT = 5 + 12 + 12 + 1 + (NX * NY - 1) + NZ // 2 + 1


def kernel(
    og_hbm, si_hbm, w_hbm, hist_ref,
    ig_out, wq_out, hist_out,
    og, si, w, ig, si_sent, og_sent, si_core, og_core,
    terms, pass_one, in_one, pass_two, in_two, ready, relay, in_last,
    peaks_core, peaks_plane, peaks_z, peaks_end, peak,
    local_sem, send_sem, recv_sem, last_send, last_recv, relay_sem, hello,
):
    dp, y = lax.axis_index("dp"), lax.axis_index("tensor")
    x, z, c = dp // (2 * NZ), lax.rem(dp // 2, NZ), lax.rem(dp, 2)
    zc, zb = lax.rem(z, 4), z // 4

    def device(x, y, z, c):
        return ((x * NZ + z) * 2 + c, y)

    def along_x(d):
        return device(lax.rem(x + d + NX, NX), y, z, c)

    def along_y(d):
        return device(x, lax.rem(y + d + NY, NY), z, c)

    def along_z(d, core=None):
        return device(x, y, lax.rem(z + d + NZ, NZ), c if core is None else core)

    def in_plane(dx, dy):
        return device(lax.rem(x + dx, NX), lax.rem(y + dy, NY), z, c)

    other_core = device(x, y, z, 1 - c)
    sides = [along_x(1), along_x(-1), along_y(1), along_y(-1)]

    def signal(sem, devices):
        for to in devices:
            pl.semaphore_signal(sem, inc=1, device_id=to, device_id_type=MESH)

    barrier = pltpu.get_barrier_semaphore()
    near = [other_core, along_z(1), along_z(-1)] + sides
    signal(barrier, near)
    rounds = [
        sides + [along_z(1), along_z(-1)],
        sides + [along_z(2), along_z(-2)],
        sides + [along_z(4), along_z(-4)],
        [along_z(8), along_z(-8)],
    ]

    def say(n):
        signal(hello.at[n], rounds[n])

    def hear(n):
        pl.semaphore_wait(hello.at[n], len(rounds[n]))

    get_og = pltpu.make_async_copy(og_hbm, og, local_sem.at[0])
    get_si = pltpu.make_async_copy(si_hbm, si, local_sem.at[1])
    get_w = pltpu.make_async_copy(w_hbm, w, local_sem.at[2])
    get_si.start()
    get_og.start()
    get_w.start()

    used = [0]
    sent = []

    def send(src, dst, to):
        n = used[0]
        used[0] += 1
        copy = pltpu.make_async_remote_copy(
            src_ref=src, dst_ref=dst, send_sem=send_sem.at[n], recv_sem=recv_sem.at[n],
            device_id=to, device_id_type=MESH,
        )
        copy.start()
        sent.append(copy)
        return copy

    scale_in = LIMIT / jnp.max(hist_ref[...])

    def group(at, i, core):
        return pl.ds(pl.multiple_of(at * 1024 + i * 256 + core * 128, 128), 128)

    get_si.wait()
    si_sent[...] = si[...].astype(F32)
    get_og.wait()
    for n, k in enumerate(ORDER):
        for i in range(4):
            og_sent[n, :, i * 128 : i * 128 + 128] = og[
                :, group(lax.rem(x + k, 4), i, 1 - c)
            ].astype(F32)
        if n == 0:
            pl.semaphore_wait(barrier, len(near))
            si_copy = send(si_sent, si_core, other_core)
            og_copies = []
        og_copies.append(send(og_sent.at[n], og_core.at[n], other_core))
    say(0)

    def quantized(grads, inputs):
        term = lax.dot_general(
            grads, inputs, (((0,), (0,)), ((), ())), preferred_element_type=F32
        )
        return jnp.clip(term * scale_in, -LIMIT, LIMIT).astype(BF16).astype(F32)

    def pieces(at, n, first):
        for i in range(2):
            for j in range(4):
                for core in range(2):
                    row = i * 128 + j * 32 + core * 16
                    yield (0, at, j, first + i, core), row
                    yield (1, j, n, first + i, core), row + 8

    def own_tile(n, k):
        at = lax.rem(x + k, 4)

        @pl.loop(0, 2)
        def _(s):
            grads = jnp.concatenate(
                [og[:, group(at, 2 * s, c)], og[:, group(at, 2 * s + 1, c)]], axis=1
            )
            quant = quantized(grads, si[...])
            for where, row in pieces(at, n, 2 * s):
                terms[where] = quant[row : row + 8]

    def other_tile(n, k):
        at = lax.rem(x + k, 4)
        og_copies[n].wait_recv()

        @pl.loop(0, 2)
        def _(s):
            columns = pl.ds(pl.multiple_of(s * 256, 256), 256)
            quant = quantized(og_core[n, :, columns].astype(BF16), si_core[...].astype(BF16))
            for where, row in pieces(at, n, 2 * s):
                terms[where] += quant[row : row + 8]

    @pl.loop(0, 4)
    def _(n):
        own_tile(n, jnp.where(n == 0, 2, jnp.where(n == 1, 1, jnp.where(n == 2, 3, 0))))

    hear(0)
    say(1)
    si_copy.wait_recv()

    A, B = pl.ds(0, 2), pl.ds(2, 2)
    plus = (along_x(1), along_z(1))
    minus = (along_x(-1), along_z(-1))
    first = (x, zc)

    def unit(p, k):
        return terms.at[p, lax.rem(first[p] + k, 4)]

    one = [{}, {}]
    other_tile(0, 2)
    one[0]["a+"] = send(unit(0, 2).at[A], pass_one.at[0, 0], plus[0])
    one[0]["a-"] = send(unit(0, 2).at[B], pass_one.at[0, 1], minus[0])
    other_tile(1, 1)
    one[1]["a+"] = send(unit(1, 2).at[A], pass_one.at[1, 0], plus[1])
    one[0]["b+"] = send(unit(0, 1).at[B], in_one.at[0, 0, B], plus[0])
    one[1]["b-"] = send(unit(1, 3).at[A], in_one.at[1, 1, A], minus[1])
    other_tile(2, 3)
    one[0]["b-"] = send(unit(0, 3).at[A], in_one.at[0, 1, A], minus[0])
    other_tile(3, 0)
    one[1]["a-"] = send(unit(1, 2).at[B], pass_one.at[1, 1], minus[1])
    one[1]["b+"] = send(unit(1, 1).at[B], in_one.at[1, 0, B], plus[1])
    hear(1)
    say(2)

    def pass_on(p, k, half, at, key_in, key_out, to):
        one[p][key_in].wait_recv()
        m = lax.rem(first[p] + k, 4)
        terms[p, m, half] += pass_one[p, at]
        one[p][key_out] = send(terms.at[p, m, half], in_one.at[p, at, half], to)

    pass_on(0, 1, A, 0, "a+", "c+", plus[0])
    pass_on(0, 3, B, 1, "a-", "c-", minus[0])
    pass_on(1, 1, A, 0, "a+", "c+", plus[1])
    pass_on(1, 3, B, 1, "a-", "c-", minus[1])

    get_w.wait()

    @pl.loop(0, 2)
    def _(i):
        rows = pl.ds(pl.multiple_of(i * 256, 256), 256)
        ig[:, rows] = lax.dot_general(
            og[...], w[rows, :], (((1,), (1,)), ((), ())), preferred_element_type=F32
        ).astype(BF16)

    put_ig = pltpu.make_async_copy(ig, ig_out, local_sem.at[3])
    put_ig.start()
    hear(2)
    say(3)

    C, D = pl.ds(0, 2), pl.ds(2, 2)
    two = [{}, {}]
    up, down = (plus[1], plus[0]), (minus[1], minus[0])

    def second(p, k):
        return lax.rem(zc + k, 4) if p == 0 else PLACE[k]

    for p in range(2):
        for key in ("b+", "b-", "c+", "c-"):
            one[p][key].wait_recv()
        m = first[p]

        def total(k):
            q = second(p, k)
            terms[p, m, q] += in_one[p, 0, q] + in_one[p, 1, q]
            return terms.at[p, m, q]

        far = total(2)
        two[p]["a+"] = send(far.at[C], pass_two.at[p, 0], up[p])
        two[p]["a-"] = send(far.at[D], pass_two.at[p, 1], down[p])
        two[p]["b+"] = send(total(1).at[D], in_two.at[p, 0, D], up[p])
        two[p]["b-"] = send(total(3).at[C], in_two.at[p, 1, C], down[p])
        total(0)
    for p in range(2):
        m = first[p]
        for key, out, k, half, at, to in (
            ("a+", "c+", 1, C, 0, up[p]),
            ("a-", "c-", 3, D, 1, down[p]),
        ):
            q = second(p, k)
            two[p][key].wait_recv()
            terms[p, m, q, half] += pass_two[p, at]
            two[p][out] = send(terms.at[p, m, q, half], in_two.at[p, at, half], to)
    for p in range(2):
        for key in ("b+", "b-", "c+", "c-"):
            two[p][key].wait_recv()
        ready[:, p] = terms[p, first[p], second(p, 0)] + in_two[p, 0] + in_two[p, 1]
    hear(3)

    even = lax.rem(zb, 2) == c

    def block(k):
        return lax.rem(zb + k, NB) // 2

    def last_copy(n, src, dst, recv, to):
        return pltpu.make_async_remote_copy(
            src_ref=src, dst_ref=dst, send_sem=last_send.at[n], recv_sem=recv,
            device_id=to, device_id_type=MESH,
        )

    def whole(n, k, core):
        return last_copy(
            n, ready.at[block(k), :, core], in_last.at[k], last_recv.at[k], along_z(4 * k, core)
        )

    def half(n, k, p, core):
        return last_copy(
            n, ready.at[block(k), p, core], in_last.at[k, p], last_recv.at[k if p == 0 else 8 + k],
            along_z(4 * k, core),
        )

    def to_relay(n, p):
        return last_copy(
            n, ready.at[block(4), p], relay.at[p], relay_sem.at[p], along_z(4 if p == 0 else -4)
        )

    def even_copies():
        return [
            to_relay(0, 0), to_relay(1, 1),
            whole(2, 2, 0), whole(3, 6, 0), whole(4, 2, 1), whole(5, 6, 1),
            last_copy(6, ready.at[block(0), :, 1 - c], in_last.at[0], last_recv.at[0], other_core),
        ]

    def odd_copies():
        return [
            half(0, 3, 1, 0), half(1, 5, 0, 0), half(2, 3, 1, 1), half(3, 5, 0, 1),
            whole(4, 1, 0), whole(5, 7, 0), whole(6, 1, 1), whole(7, 7, 1),
        ]

    def odd_passed(p):
        k = 3 if p == 0 else 5
        return [half(8 + 2 * p, k, p, 0), half(9 + 2 * p, k, p, 1)]

    @pl.when(even)
    def _():
        for copy in even_copies():
            copy.start()
        in_last[0] = ready[zb // 2, :, c]

    @pl.when(jnp.logical_not(even))
    def _():
        for copy in odd_copies():
            copy.start()
        for p, k in ((0, 3), (1, 5)):
            to_relay(0, p).wait_recv()
            ready[block(k), p] += relay[p]
            for copy in odd_passed(p):
                copy.start()
        last_copy(0, in_last.at[0], in_last.at[0], last_recv.at[0], other_core).wait_recv()

    summed = in_last[0]
    for k in (1, 7, 2, 6):
        whole(0, k, 0).wait_recv()
        summed = summed + in_last[k]
    for k in (3, 5):
        for p in range(2):
            half(0, k, p, 0).wait_recv()
        summed = summed + in_last[k]
    weight_sum = summed / scale_in

    one_row = pl.ds(0, 1)

    def put_peak(n, value):
        peak[n, 0:1, :] = value

    top = jnp.max(jnp.max(jnp.abs(weight_sum), axis=0), axis=0, keepdims=True)
    best = top[:, 0:128]
    for i in range(1, 4):
        best = jnp.maximum(best, top[:, i * 128 : i * 128 + 128])
    put_peak(0, best)
    send(peak.at[0, one_row], peaks_core.at[one_row], other_core).wait_recv()
    best = jnp.maximum(best, peaks_core[0:1, :])
    put_peak(1, best)
    plane = [
        send(peak.at[1, one_row], peaks_plane.at[d, one_row], in_plane(d // NY, d % NY))
        for d in range(1, NX * NY)
    ]
    for d, copy in enumerate(plane, 1):
        copy.wait_recv()
        best = jnp.maximum(best, peaks_plane[d, 0:1, :])
    put_peak(2, best)
    way = 1 - 2 * c
    ring = [
        send(peak.at[2, one_row], peaks_z.at[k - 1, one_row], along_z(way * k))
        for k in range(NZ // 2, 0, -1)
    ]
    for k, copy in zip(range(NZ // 2, 0, -1), ring):
        copy.wait_recv()
        best = jnp.maximum(best, peaks_z[k - 1, 0:1, :])
    put_peak(3, best)
    send(peak.at[3, one_row], peaks_end.at[one_row], other_core).wait_recv()
    amax = jnp.max(jnp.maximum(best, peaks_end[0:1, :]), axis=1, keepdims=True)

    lane = lax.broadcasted_iota(jnp.int32, (1, 16), 1)
    new_history = jnp.where(lane == 0, amax, jnp.roll(hist_ref[...], 1, axis=1))
    hist_out[...] = new_history
    out_scale = LIMIT / jnp.max(new_history)
    wq_out[...] = (weight_sum * out_scale).reshape(16, 512)

    for copy in sent:
        copy.wait_send()

    @pl.when(even)
    def _():
        for copy in even_copies():
            copy.wait_send()

    @pl.when(jnp.logical_not(even))
    def _():
        for copy in odd_copies() + odd_passed(0) + odd_passed(1):
            copy.wait_send()

    put_ig.wait()


def write_out(ig_in, wq_in, hist_in, ig_out, wq_out, hist_out, sem):
    copy = pltpu.make_async_copy(ig_in, ig_out, sem)
    copy.start()
    wq_out[...] = wq_in[...].astype(BF16)
    hist_out[...] = hist_in[...]
    copy.wait()


def shards(out_grad, saved_input, weight, amax_history):
    any_space = pl.BlockSpec(memory_space=pl.ANY)
    vmem = pl.BlockSpec(memory_space=pltpu.VMEM)
    part = (8, 512)
    input_grad, weight_q, history = pl.pallas_call(
        kernel,
        out_shape=(
            jax.ShapeDtypeStruct((192, 512), BF16),
            jax.ShapeDtypeStruct((16, 512), F32),
            jax.ShapeDtypeStruct((1, 16), F32),
        ),
        in_specs=[any_space, any_space, any_space, vmem],
        out_specs=[any_space, vmem, vmem],
        scratch_shapes=[
            pltpu.VMEM((192, 4096), BF16),
            pltpu.VMEM((192, 512), BF16),
            pltpu.VMEM((512, 4096), BF16),
            pltpu.VMEM((192, 512), BF16),
            pltpu.VMEM((192, 512), F32),
            pltpu.VMEM((4, 192, 512), F32),
            pltpu.VMEM((192, 512), F32),
            pltpu.VMEM((4, 192, 512), F32),
            pltpu.VMEM((2, 4, 4, 4, 2) + part, F32),
            pltpu.VMEM((2, 2, 2, 4, 2) + part, F32),
            pltpu.VMEM((2, 2, 4, 4, 2) + part, F32),
            pltpu.VMEM((2, 2, 2, 2) + part, F32),
            pltpu.VMEM((2, 2, 4, 2) + part, F32),
            pltpu.VMEM((4, 2, 2) + part, F32),
            pltpu.VMEM((2, 2) + part, F32),
            pltpu.VMEM((NB, 2) + part, F32),
            pltpu.VMEM((8, 128), F32),
            pltpu.VMEM((NX * NY, 8, 128), F32),
            pltpu.VMEM((NZ // 2, 8, 128), F32),
            pltpu.VMEM((8, 128), F32),
            pltpu.VMEM((4, 8, 128), F32),
            pltpu.SemaphoreType.DMA((4,)),
            pltpu.SemaphoreType.DMA((N_SENT,)),
            pltpu.SemaphoreType.DMA((N_SENT,)),
            pltpu.SemaphoreType.DMA((12,)),
            pltpu.SemaphoreType.DMA((16,)),
            pltpu.SemaphoreType.DMA((2,)),
            pltpu.SemaphoreType.REGULAR((4,)),
        ],
        compiler_params=pltpu.CompilerParams(
            collective_id=0, has_side_effects=True, vmem_limit_bytes=60 * 2**20
        ),
        name="all_steps",
    )(out_grad, saved_input, weight, amax_history.reshape(1, 16))
    input_grad, weight_q, history = pl.pallas_call(
        write_out,
        out_shape=(
            jax.ShapeDtypeStruct((192, 512), BF16),
            jax.ShapeDtypeStruct((16, 512), BF16),
            jax.ShapeDtypeStruct((1, 16), F32),
        ),
        in_specs=[any_space, vmem, vmem],
        out_specs=[any_space, vmem, vmem],
        scratch_shapes=[pltpu.SemaphoreType.DMA],
        compiler_params=pltpu.CompilerParams(vmem_limit_bytes=60 * 2**20),
        name="write_out",
    )(input_grad, weight_q, history)
    return (input_grad, weight_q.T, history.reshape(16))


def solution(mesh):
    placed = (P("dp", None), P("dp", "tensor"), P("tensor", None), P())
    return jax.shard_map(
        shards,
        mesh=mesh,
        in_specs=placed,
        out_specs=(P("dp", "tensor"), P("tensor", "dp"), P()),
        check_vma=False,
    )
```

```python
import jax
import jax.numpy as jnp
from jax import lax
from jax.experimental import pallas as pl
from jax.experimental.pallas import tpu as pltpu
from jax.sharding import PartitionSpec as P

LIMIT = 8.0
MESH = pl.DeviceIdType.MESH
NX, NZ, NY = 4, 32, 4
NB = NZ // 4
F32, BF16 = jnp.float32, jnp.bfloat16
ORDER = (2, 1, 3, 0)
PLACE = {k: n for n, k in enumerate(ORDER)}
N_SENT = 5 + 12 + 12 + (2 * NX * NY - 1) + NZ // 2 + 1


def kernel(
    og_hbm, si_hbm, w_hbm, hist_ref,
    ig_out, wq_out, hist_out,
    og, si, w, ig, si_sent, og_sent, si_core, og_core, si_other,
    terms, pass_one, in_one, pass_two, in_two, ready, relay, relay_far, in_last,
    peaks_plane, peaks_z, peaks_end, peak,
    local_sem, send_sem, recv_sem, last_send, last_recv, relay_sem, hello,
):
    dp, y = lax.axis_index("dp"), lax.axis_index("tensor")
    x, z, c = dp // (2 * NZ), lax.rem(dp // 2, NZ), lax.rem(dp, 2)
    zc, zb = lax.rem(z, 4), z // 4

    def device(x, y, z, c):
        return ((x * NZ + z) * 2 + c, y)

    def along_x(d):
        return device(lax.rem(x + d + NX, NX), y, z, c)

    def along_y(d):
        return device(x, lax.rem(y + d + NY, NY), z, c)

    def along_z(d, core=None):
        return device(x, y, lax.rem(z + d + NZ, NZ), c if core is None else core)

    def in_plane(dx, dy, dc):
        return device(lax.rem(x + dx, NX), lax.rem(y + dy, NY), z, lax.rem(c + dc, 2))

    other_core = device(x, y, z, 1 - c)
    sides = [along_x(1), along_x(-1), along_y(1), along_y(-1)]

    def signal(sem, devices):
        for to in devices:
            pl.semaphore_signal(sem, inc=1, device_id=to, device_id_type=MESH)

    barrier = pltpu.get_barrier_semaphore()
    near = [other_core, along_z(1), along_z(-1)] + sides
    signal(barrier, near)
    rounds = [
        sides + [along_z(1), along_z(-1)],
        sides + [along_z(2), along_z(-2)],
        sides + [along_z(4), along_z(-4)],
        [along_z(8), along_z(-8)],
    ]

    def say(n):
        signal(hello.at[n], rounds[n])

    def hear(n):
        pl.semaphore_wait(hello.at[n], len(rounds[n]))

    def columns_of(k):
        return pl.ds(pl.multiple_of(lax.rem(x + k, 4) * 1024, 1024), 1024)

    get_si = pltpu.make_async_copy(si_hbm, si, local_sem.at[0])
    get_og = [
        pltpu.make_async_copy(
            og_hbm.at[:, columns_of(k)], og.at[:, columns_of(k)], local_sem.at[1 + n]
        )
        for n, k in enumerate(ORDER)
    ]
    get_w = pltpu.make_async_copy(w_hbm, w, local_sem.at[5])
    get_si.start()
    for copy in get_og:
        copy.start()

    used = [0]
    sent = []

    def send(src, dst, to):
        n = used[0]
        used[0] += 1
        copy = pltpu.make_async_remote_copy(
            src_ref=src, dst_ref=dst, send_sem=send_sem.at[n], recv_sem=recv_sem.at[n],
            device_id=to, device_id_type=MESH,
        )
        copy.start()
        sent.append(copy)
        return copy

    scale_in = LIMIT / jnp.max(hist_ref[...])

    def group(at, i, core):
        return pl.ds(pl.multiple_of(at * 1024 + i * 256 + core * 128, 128), 128)

    get_si.wait()
    si_sent[...] = si[...].astype(F32)
    og_copies = []
    for n, k in enumerate(ORDER):
        get_og[n].wait()
        for i in range(4):
            og_sent[n, :, i * 128 : i * 128 + 128] = og[
                :, group(lax.rem(x + k, 4), i, 1 - c)
            ].astype(F32)
        if n == 0:
            pl.semaphore_wait(barrier, len(near))
            si_copy = send(si_sent, si_core, other_core)
        og_copies.append(send(og_sent.at[n], og_core.at[n], other_core))
    get_w.start()
    say(0)

    def quantized(grads, inputs):
        term = lax.dot_general(
            grads, inputs, (((0,), (0,)), ((), ())), preferred_element_type=F32
        )
        return jnp.clip(term * scale_in, -LIMIT, LIMIT).astype(BF16).astype(F32)

    def pieces(at, n, first):
        for i in range(2):
            for j in range(4):
                for core in range(2):
                    row = i * 128 + j * 32 + core * 16
                    yield (0, at, j, first + i, core), row
                    yield (1, j, n, first + i, core), row + 8

    def own_tile(n, k):
        at = lax.rem(x + k, 4)

        @pl.loop(0, 2)
        def _(s):
            grads = jnp.concatenate(
                [og[:, group(at, 2 * s, c)], og[:, group(at, 2 * s + 1, c)]], axis=1
            )
            quant = quantized(grads, si[...])
            for where, row in pieces(at, n, 2 * s):
                terms[where] = quant[row : row + 8]

    def other_tile(n, k):
        at = lax.rem(x + k, 4)
        if n == 0:
            si_copy.wait_recv()
            si_other[...] = si_core[...].astype(BF16)
        og_copies[n].wait_recv()

        @pl.loop(0, 2)
        def _(s):
            columns = pl.ds(pl.multiple_of(s * 256, 256), 256)
            quant = quantized(og_core[n, :, columns].astype(BF16), si_other[...])
            for where, row in pieces(at, n, 2 * s):
                terms[where] += quant[row : row + 8]

    A, B = pl.ds(0, 2), pl.ds(2, 2)
    plus = (along_x(1), along_z(1))
    minus = (along_x(-1), along_z(-1))
    first = (x, zc)

    def unit(p, k):
        return terms.at[p, lax.rem(first[p] + k, 4)]

    one = [{}, {}]
    own_tile(0, 2)
    other_tile(0, 2)
    one[0]["a+"] = send(unit(0, 2).at[A], pass_one.at[0, 0], plus[0])
    one[0]["a-"] = send(unit(0, 2).at[B], pass_one.at[0, 1], minus[0])
    hear(0)
    say(1)
    own_tile(1, 1)
    other_tile(1, 1)
    one[1]["a+"] = send(unit(1, 2).at[A], pass_one.at[1, 0], plus[1])
    one[0]["b+"] = send(unit(0, 1).at[B], in_one.at[0, 0, B], plus[0])
    one[1]["b-"] = send(unit(1, 3).at[A], in_one.at[1, 1, A], minus[1])
    own_tile(2, 3)
    other_tile(2, 3)
    one[0]["b-"] = send(unit(0, 3).at[A], in_one.at[0, 1, A], minus[0])
    own_tile(3, 0)
    other_tile(3, 0)
    one[1]["a-"] = send(unit(1, 2).at[B], pass_one.at[1, 1], minus[1])
    one[1]["b+"] = send(unit(1, 1).at[B], in_one.at[1, 0, B], plus[1])
    hear(1)
    say(2)

    def pass_on(p, k, half, at, key_in, key_out, to):
        one[p][key_in].wait_recv()
        m = lax.rem(first[p] + k, 4)
        terms[p, m, half] += pass_one[p, at]
        one[p][key_out] = send(terms.at[p, m, half], in_one.at[p, at, half], to)

    pass_on(0, 1, A, 0, "a+", "c+", plus[0])
    pass_on(0, 3, B, 1, "a-", "c-", minus[0])
    pass_on(1, 1, A, 0, "a+", "c+", plus[1])
    pass_on(1, 3, B, 1, "a-", "c-", minus[1])

    get_w.wait()

    @pl.loop(0, 2)
    def _(i):
        rows = pl.ds(pl.multiple_of(i * 256, 256), 256)
        ig[:, rows] = lax.dot_general(
            og[...], w[rows, :], (((1,), (1,)), ((), ())), preferred_element_type=F32
        ).astype(BF16)

    put_ig = pltpu.make_async_copy(ig, ig_out, local_sem.at[6])
    put_ig.start()
    hear(2)
    say(3)

    C, D = pl.ds(0, 2), pl.ds(2, 2)
    two = [{}, {}]
    up, down = (plus[1], plus[0]), (minus[1], minus[0])

    def second(p, k):
        return lax.rem(zc + k, 4) if p == 0 else PLACE[k]

    for p in range(2):
        for key in ("b+", "b-", "c+", "c-"):
            one[p][key].wait_recv()
        m = first[p]

        def total(k):
            q = second(p, k)
            terms[p, m, q] += in_one[p, 0, q] + in_one[p, 1, q]
            return terms.at[p, m, q]

        far = total(2)
        two[p]["a+"] = send(far.at[C], pass_two.at[p, 0], up[p])
        two[p]["a-"] = send(far.at[D], pass_two.at[p, 1], down[p])
        two[p]["b+"] = send(total(1).at[D], in_two.at[p, 0, D], up[p])
        two[p]["b-"] = send(total(3).at[C], in_two.at[p, 1, C], down[p])
        total(0)
    for p in range(2):
        m = first[p]
        for key, out, k, half, at, to in (
            ("a+", "c+", 1, C, 0, up[p]),
            ("a-", "c-", 3, D, 1, down[p]),
        ):
            q = second(p, k)
            two[p][key].wait_recv()
            terms[p, m, q, half] += pass_two[p, at]
            two[p][out] = send(terms.at[p, m, q, half], in_two.at[p, at, half], to)
    for p in range(2):
        for key in ("b+", "b-", "c+", "c-"):
            two[p][key].wait_recv()
        ready[:, p] = terms[p, first[p], second(p, 0)] + in_two[p, 0] + in_two[p, 1]
    hear(3)

    even = lax.rem(zb, 2) == c

    def block(k):
        return lax.rem(zb + k, NB) // 2

    def last_copy(n, src, dst, recv, to):
        return pltpu.make_async_remote_copy(
            src_ref=src, dst_ref=dst, send_sem=last_send.at[n], recv_sem=recv,
            device_id=to, device_id_type=MESH,
        )

    def whole(n, k, core):
        return last_copy(
            n, ready.at[block(k), :, core], in_last.at[k], last_recv.at[k], along_z(4 * k, core)
        )

    def relay_half(n, p):
        return last_copy(
            n, ready.at[block(4), p], relay_far.at[p], relay_sem.at[p], along_z(8 if p == 0 else -8)
        )

    def relay_whole(n, k):
        at = 0 if k == 3 else 1
        return last_copy(
            n, ready.at[block(k)], relay.at[at], relay_sem.at[2 + at], along_z(4 if k == 3 else -4)
        )

    def even_first():
        to_core = last_copy(
            2, ready.at[block(0), :, 1 - c], in_last.at[0], last_recv.at[0], other_core
        )
        return [relay_half(0, 0), relay_half(1, 1), to_core]

    def even_then(k):
        return [whole(1 + k, k, 0), whole(2 + k, k, 1)]

    def odd_copies():
        return [
            relay_whole(0, 3), relay_whole(1, 5),
            whole(2, 1, 0), whole(3, 7, 0), whole(4, 1, 1), whole(5, 7, 1),
        ]

    @pl.when(even)
    def _():
        for copy in even_first():
            copy.start()
        in_last[0] = ready[zb // 2, :, c]
        for p, k in ((0, 2), (1, 6)):
            relay_whole(0, 3 if p == 0 else 5).wait_recv()
            ready[block(k)] += relay[p]
            relay_half(0, p).wait_recv()
            ready[block(k), p] += relay_far[p]
            for copy in even_then(k):
                copy.start()

    @pl.when(jnp.logical_not(even))
    def _():
        for copy in odd_copies():
            copy.start()
        last_copy(0, in_last.at[0], in_last.at[0], last_recv.at[0], other_core).wait_recv()

    summed = in_last[0]
    for k in (1, 7, 2, 6):
        whole(0, k, 0).wait_recv()
        summed = summed + in_last[k]
    weight_sum = summed / scale_in

    one_row = pl.ds(0, 1)

    def put_peak(n, value):
        peak[n, 0:1, :] = value

    top = jnp.max(jnp.max(jnp.abs(weight_sum), axis=0), axis=0, keepdims=True)
    best = top[:, 0:128]
    for i in range(1, 4):
        best = jnp.maximum(best, top[:, i * 128 : i * 128 + 128])
    put_peak(1, best)
    plane = [
        send(peak.at[1, one_row], peaks_plane.at[d, one_row], in_plane(d // 2 // NY, d // 2 % NY, d % 2))
        for d in range(1, 2 * NX * NY)
    ]
    for d, copy in enumerate(plane, 1):
        copy.wait_recv()
        best = jnp.maximum(best, peaks_plane[d, 0:1, :])
    put_peak(2, best)
    way = 1 - 2 * c
    ring = [
        send(peak.at[2, one_row], peaks_z.at[k - 1, one_row], along_z(way * k))
        for k in range(NZ // 2, 0, -1)
    ]
    for k, copy in zip(range(NZ // 2, 0, -1), ring):
        copy.wait_recv()
        best = jnp.maximum(best, peaks_z[k - 1, 0:1, :])
    put_peak(3, best)
    send(peak.at[3, one_row], peaks_end.at[one_row], other_core).wait_recv()
    amax = jnp.max(jnp.maximum(best, peaks_end[0:1, :]), axis=1, keepdims=True)

    lane = lax.broadcasted_iota(jnp.int32, (1, 16), 1)
    new_history = jnp.where(lane == 0, amax, jnp.roll(hist_ref[...], 1, axis=1))
    hist_out[...] = new_history
    out_scale = LIMIT / jnp.max(new_history)
    wq_out[...] = (weight_sum * out_scale).reshape(16, 512)

    for copy in sent:
        copy.wait_send()

    @pl.when(even)
    def _():
        for copy in even_first() + even_then(2) + even_then(6):
            copy.wait_send()

    @pl.when(jnp.logical_not(even))
    def _():
        for copy in odd_copies():
            copy.wait_send()

    put_ig.wait()


def write_out(ig_in, wq_in, hist_in, ig_out, wq_out, hist_out):
    ig_out[...] = ig_in[...]
    wq_out[...] = wq_in[...].astype(BF16)
    hist_out[...] = hist_in[...]


def shards(out_grad, saved_input, weight, amax_history):
    any_space = pl.BlockSpec(memory_space=pl.ANY)
    vmem = pl.BlockSpec(memory_space=pltpu.VMEM)
    part = (8, 512)
    input_grad, weight_q, history = pl.pallas_call(
        kernel,
        out_shape=(
            jax.ShapeDtypeStruct((192, 512), BF16),
            jax.ShapeDtypeStruct((16, 512), F32),
            jax.ShapeDtypeStruct((1, 16), F32),
        ),
        in_specs=[any_space, any_space, any_space, vmem],
        out_specs=[any_space, vmem, vmem],
        scratch_shapes=[
            pltpu.VMEM((192, 4096), BF16),
            pltpu.VMEM((192, 512), BF16),
            pltpu.VMEM((512, 4096), BF16),
            pltpu.VMEM((192, 512), BF16),
            pltpu.VMEM((192, 512), F32),
            pltpu.VMEM((4, 192, 512), F32),
            pltpu.VMEM((192, 512), F32),
            pltpu.VMEM((4, 192, 512), F32),
            pltpu.VMEM((192, 512), BF16),
            pltpu.VMEM((2, 4, 4, 4, 2) + part, F32),
            pltpu.VMEM((2, 2, 2, 4, 2) + part, F32),
            pltpu.VMEM((2, 2, 4, 4, 2) + part, F32),
            pltpu.VMEM((2, 2, 2, 2) + part, F32),
            pltpu.VMEM((2, 2, 4, 2) + part, F32),
            pltpu.VMEM((4, 2, 2) + part, F32),
            pltpu.VMEM((2, 2, 2) + part, F32),
            pltpu.VMEM((2, 2) + part, F32),
            pltpu.VMEM((NB, 2) + part, F32),
            pltpu.VMEM((2 * NX * NY, 8, 128), F32),
            pltpu.VMEM((NZ // 2, 8, 128), F32),
            pltpu.VMEM((8, 128), F32),
            pltpu.VMEM((4, 8, 128), F32),
            pltpu.SemaphoreType.DMA((7,)),
            pltpu.SemaphoreType.DMA((N_SENT,)),
            pltpu.SemaphoreType.DMA((N_SENT,)),
            pltpu.SemaphoreType.DMA((9,)),
            pltpu.SemaphoreType.DMA((NB,)),
            pltpu.SemaphoreType.DMA((4,)),
            pltpu.SemaphoreType.REGULAR((4,)),
        ],
        compiler_params=pltpu.CompilerParams(
            collective_id=0, has_side_effects=True, vmem_limit_bytes=60 * 2**20
        ),
        name="all_steps",
    )(out_grad, saved_input, weight, amax_history.reshape(1, 16))
    input_grad, weight_q, history = pl.pallas_call(
        write_out,
        out_shape=(
            jax.ShapeDtypeStruct((192, 512), BF16),
            jax.ShapeDtypeStruct((16, 512), BF16),
            jax.ShapeDtypeStruct((1, 16), F32),
        ),
        in_specs=[vmem, vmem, vmem],
        out_specs=[vmem, vmem, vmem],
        compiler_params=pltpu.CompilerParams(vmem_limit_bytes=60 * 2**20),
        name="write_out",
    )(input_grad, weight_q, history)
    return (input_grad, weight_q.T, history.reshape(16))


def solution(mesh):
    placed = (P("dp", None), P("dp", "tensor"), P("tensor", None), P())
    return jax.shard_map(
        shards,
        mesh=mesh,
        in_specs=placed,
        out_specs=(P("dp", "tensor"), P("tensor", "dp"), P()),
        check_vma=False,
    )
```

```python
import jax
import jax.numpy as jnp
from jax import lax
from jax.experimental import pallas as pl
from jax.experimental.pallas import tpu as pltpu
from jax.sharding import PartitionSpec as P

LIMIT = 8.0
MESH = pl.DeviceIdType.MESH
NX, NZ, NY = 4, 32, 4
NB = NZ // 4
F32, BF16 = jnp.float32, jnp.bfloat16
ORDER = (2, 1, 3, 0)
PLACE = {k: n for n, k in enumerate(ORDER)}
N_SENT = 5 + 12 + 12 + (2 * NX * NY - 1) + NZ // 2 + 1


def kernel(
    og_hbm, si_hbm, w_hbm, hist_ref,
    ig_out, wq_out, hist_out,
    og, si, w, ig, si_sent, og_sent, si_core, og_core, si_other,
    terms, pass_one, in_one, pass_two, in_two, ready, relay, relay_far, in_last,
    peaks_plane, peaks_z, peaks_end, peak,
    local_sem, send_sem, recv_sem, last_send, last_recv, relay_sem, hello,
):
    dp, y = lax.axis_index("dp"), lax.axis_index("tensor")
    x, z, c = dp // (2 * NZ), lax.rem(dp // 2, NZ), lax.rem(dp, 2)
    zc, zb = lax.rem(z, 4), z // 4

    def device(x, y, z, c):
        return ((x * NZ + z) * 2 + c, y)

    def along_x(d):
        return device(lax.rem(x + d + NX, NX), y, z, c)

    def along_y(d):
        return device(x, lax.rem(y + d + NY, NY), z, c)

    def along_z(d, core=None):
        return device(x, y, lax.rem(z + d + NZ, NZ), c if core is None else core)

    def in_plane(dx, dy, dc):
        return device(lax.rem(x + dx, NX), lax.rem(y + dy, NY), z, lax.rem(c + dc, 2))

    other_core = device(x, y, z, 1 - c)
    sides = [along_x(1), along_x(-1), along_y(1), along_y(-1)]

    def signal(sem, devices):
        for to in devices:
            pl.semaphore_signal(sem, inc=1, device_id=to, device_id_type=MESH)

    barrier = pltpu.get_barrier_semaphore()
    near = [other_core, along_z(1), along_z(-1)] + sides
    signal(barrier, near)
    rounds = [
        sides + [along_z(1), along_z(-1)],
        sides + [along_z(2), along_z(-2)],
        sides + [along_z(4), along_z(-4)],
        [along_z(8), along_z(-8)],
    ]

    def say(n):
        signal(hello.at[n], rounds[n])

    def hear(n):
        pl.semaphore_wait(hello.at[n], len(rounds[n]))

    def columns_of(k):
        return pl.ds(pl.multiple_of(lax.rem(x + k, 4) * 1024, 1024), 1024)

    get_si = pltpu.make_async_copy(si_hbm, si, local_sem.at[0])
    get_og = [
        pltpu.make_async_copy(
            og_hbm.at[:, columns_of(k)], og.at[:, columns_of(k)], local_sem.at[1 + n]
        )
        for n, k in enumerate(ORDER)
    ]
    get_w = pltpu.make_async_copy(w_hbm, w, local_sem.at[5])
    get_si.start()
    for copy in get_og:
        copy.start()

    used = [0]
    sent = []

    def send(src, dst, to):
        n = used[0]
        used[0] += 1
        copy = pltpu.make_async_remote_copy(
            src_ref=src, dst_ref=dst, send_sem=send_sem.at[n], recv_sem=recv_sem.at[n],
            device_id=to, device_id_type=MESH,
        )
        copy.start()
        sent.append(copy)
        return copy

    def left(copy):
        copy.wait_send()
        sent[:] = [other for other in sent if other is not copy]

    scale_in = LIMIT / jnp.max(hist_ref[...])

    def group(at, i, core):
        return pl.ds(pl.multiple_of(at * 1024 + i * 256 + core * 128, 128), 128)

    get_si.wait()
    si_sent[...] = si[...].astype(F32)
    og_copies = []
    for n, k in enumerate(ORDER):
        get_og[n].wait()
        for i in range(4):
            og_sent[n, :, i * 128 : i * 128 + 128] = og[
                :, group(lax.rem(x + k, 4), i, 1 - c)
            ].astype(F32)
        if n == 0:
            pl.semaphore_wait(barrier, len(near))
            si_copy = send(si_sent, si_core, other_core)
        og_copies.append(send(og_sent.at[n], og_core.at[n], other_core))
    get_w.start()
    say(0)

    def quantized(grads, inputs):
        term = lax.dot_general(
            grads, inputs, (((0,), (0,)), ((), ())), preferred_element_type=F32
        )
        return jnp.clip(term * scale_in, -LIMIT, LIMIT).astype(BF16).astype(F32)

    def pieces(at, n, first):
        for i in range(2):
            for j in range(4):
                for core in range(2):
                    row = i * 128 + j * 32 + core * 16
                    yield (0, at, j, first + i, core), row
                    yield (1, j, n, first + i, core), row + 8

    def own_tile(n, k):
        at = lax.rem(x + k, 4)

        @pl.loop(0, 2)
        def _(s):
            grads = jnp.concatenate(
                [og[:, group(at, 2 * s, c)], og[:, group(at, 2 * s + 1, c)]], axis=1
            )
            quant = quantized(grads, si[...])
            for where, row in pieces(at, n, 2 * s):
                terms[where] = quant[row : row + 8]

    def other_tile(n, k):
        at = lax.rem(x + k, 4)
        if n == 0:
            si_copy.wait_recv()
            si_other[...] = si_core[...].astype(BF16)
        og_copies[n].wait_recv()

        @pl.loop(0, 2)
        def _(s):
            columns = pl.ds(pl.multiple_of(s * 256, 256), 256)
            quant = quantized(og_core[n, :, columns].astype(BF16), si_other[...])
            for where, row in pieces(at, n, 2 * s):
                terms[where] += quant[row : row + 8]

    A, B = pl.ds(0, 2), pl.ds(2, 2)
    plus = (along_x(1), along_z(1))
    minus = (along_x(-1), along_z(-1))
    first = (x, zc)

    def unit(p, k):
        return terms.at[p, lax.rem(first[p] + k, 4)]

    one = [{}, {}]
    own_tile(0, 2)
    other_tile(0, 2)
    one[0]["a+"] = send(unit(0, 2).at[A], pass_one.at[0, 0], plus[0])
    one[0]["a-"] = send(unit(0, 2).at[B], pass_one.at[0, 1], minus[0])
    hear(0)
    say(1)
    own_tile(1, 1)
    other_tile(1, 1)
    one[1]["a+"] = send(unit(1, 2).at[A], pass_one.at[1, 0], plus[1])
    own_tile(2, 3)
    other_tile(2, 3)
    own_tile(3, 0)
    other_tile(3, 0)
    one[1]["a-"] = send(unit(1, 2).at[B], pass_one.at[1, 1], minus[1])
    hear(1)
    say(2)

    def pass_on(p, k, half, at, key_in, key_out, to):
        one[p][key_in].wait_recv()
        m = lax.rem(first[p] + k, 4)
        terms[p, m, half] += pass_one[p, at]
        one[p][key_out] = send(terms.at[p, m, half], in_one.at[p, at, half], to)

    def direct(p, sign):
        left(one[p]["a" + sign])
        if sign == "+":
            one[p]["b+"] = send(unit(p, 1).at[B], in_one.at[p, 0, B], plus[p])
        else:
            one[p]["b-"] = send(unit(p, 3).at[A], in_one.at[p, 1, A], minus[p])

    direct(0, "+")
    direct(0, "-")
    direct(1, "+")
    pass_on(0, 1, A, 0, "a+", "c+", plus[0])
    pass_on(0, 3, B, 1, "a-", "c-", minus[0])
    direct(1, "-")
    pass_on(1, 1, A, 0, "a+", "c+", plus[1])
    pass_on(1, 3, B, 1, "a-", "c-", minus[1])

    get_w.wait()

    @pl.loop(0, 2)
    def _(i):
        rows = pl.ds(pl.multiple_of(i * 256, 256), 256)
        ig[:, rows] = lax.dot_general(
            og[...], w[rows, :], (((1,), (1,)), ((), ())), preferred_element_type=F32
        ).astype(BF16)

    put_ig = pltpu.make_async_copy(ig, ig_out, local_sem.at[6])
    put_ig.start()
    hear(2)
    say(3)

    C, D = pl.ds(0, 2), pl.ds(2, 2)
    two = [{}, {}]
    up, down = (plus[1], plus[0]), (minus[1], minus[0])

    def second(p, k):
        return lax.rem(zc + k, 4) if p == 0 else PLACE[k]

    def total(p, k):
        m, q = first[p], second(p, k)
        terms[p, m, q] += in_one[p, 0, q] + in_one[p, 1, q]
        return terms.at[p, m, q]

    for p in range(2):
        for key in ("b+", "b-", "c+", "c-"):
            one[p][key].wait_recv()
        far = total(p, 2)
        two[p]["a+"] = send(far.at[C], pass_two.at[p, 0], up[p])
        two[p]["a-"] = send(far.at[D], pass_two.at[p, 1], down[p])
    for p in range(2):
        near_up, near_down = total(p, 1), total(p, 3)
        left(two[p]["a+"])
        two[p]["b+"] = send(near_up.at[D], in_two.at[p, 0, D], up[p])
        left(two[p]["a-"])
        two[p]["b-"] = send(near_down.at[C], in_two.at[p, 1, C], down[p])
        total(p, 0)
    for p in range(2):
        m = first[p]
        for key, out, k, half, at, to in (
            ("a+", "c+", 1, C, 0, up[p]),
            ("a-", "c-", 3, D, 1, down[p]),
        ):
            q = second(p, k)
            two[p][key].wait_recv()
            terms[p, m, q, half] += pass_two[p, at]
            two[p][out] = send(terms.at[p, m, q, half], in_two.at[p, at, half], to)
    for p in range(2):
        for key in ("b+", "b-", "c+", "c-"):
            two[p][key].wait_recv()
        ready[:, p] = terms[p, first[p], second(p, 0)] + in_two[p, 0] + in_two[p, 1]
    hear(3)

    even = lax.rem(zb, 2) == c

    def block(k):
        return lax.rem(zb + k, NB) // 2

    def last_copy(n, src, dst, recv, to):
        return pltpu.make_async_remote_copy(
            src_ref=src, dst_ref=dst, send_sem=last_send.at[n], recv_sem=recv,
            device_id=to, device_id_type=MESH,
        )

    def whole(n, k, core):
        return last_copy(
            n, ready.at[block(k), :, core], in_last.at[k], last_recv.at[k], along_z(4 * k, core)
        )

    def relay_half(n, p):
        return last_copy(
            n, ready.at[block(4), p], relay_far.at[p], relay_sem.at[p], along_z(8 if p == 0 else -8)
        )

    def relay_whole(n, k):
        at = 0 if k == 3 else 1
        return last_copy(
            n, ready.at[block(k)], relay.at[at], relay_sem.at[2 + at], along_z(4 if k == 3 else -4)
        )

    def even_first():
        to_core = last_copy(
            2, ready.at[block(0), :, 1 - c], in_last.at[0], last_recv.at[0], other_core
        )
        return [relay_half(0, 0), relay_half(1, 1), to_core]

    def even_then(k):
        return [whole(1 + k, k, 0), whole(2 + k, k, 1)]

    def odd_first():
        return [relay_whole(0, 3), relay_whole(1, 5)]

    def odd_then():
        return [whole(2, 1, 0), whole(3, 7, 0), whole(4, 1, 1), whole(5, 7, 1)]

    @pl.when(even)
    def _():
        for copy in even_first():
            copy.start()
        in_last[0] = ready[zb // 2, :, c]
        for p, k in ((0, 2), (1, 6)):
            relay_whole(0, 3 if p == 0 else 5).wait_recv()
            ready[block(k)] += relay[p]
            relay_half(0, p).wait_recv()
            ready[block(k), p] += relay_far[p]
            for copy in even_then(k):
                copy.start()

    @pl.when(jnp.logical_not(even))
    def _():
        for copy in odd_first():
            copy.start()
        for copy in odd_first():
            copy.wait_send()
        for copy in odd_then():
            copy.start()
        last_copy(0, in_last.at[0], in_last.at[0], last_recv.at[0], other_core).wait_recv()

    summed = in_last[0]
    for k in (1, 7, 2, 6):
        whole(0, k, 0).wait_recv()
        summed = summed + in_last[k]
    weight_sum = summed / scale_in

    one_row = pl.ds(0, 1)

    def put_peak(n, value):
        peak[n, 0:1, :] = value

    top = jnp.max(jnp.max(jnp.abs(weight_sum), axis=0), axis=0, keepdims=True)
    best = top[:, 0:128]
    for i in range(1, 4):
        best = jnp.maximum(best, top[:, i * 128 : i * 128 + 128])
    put_peak(1, best)
    plane = [
        send(peak.at[1, one_row], peaks_plane.at[d, one_row], in_plane(d // 2 // NY, d // 2 % NY, d % 2))
        for d in range(1, 2 * NX * NY)
    ]
    for d, copy in enumerate(plane, 1):
        copy.wait_recv()
        best = jnp.maximum(best, peaks_plane[d, 0:1, :])
    put_peak(2, best)
    way = 1 - 2 * c
    ring = [
        send(peak.at[2, one_row], peaks_z.at[k - 1, one_row], along_z(way * k))
        for k in range(NZ // 2, 0, -1)
    ]
    for k, copy in zip(range(NZ // 2, 0, -1), ring):
        copy.wait_recv()
        best = jnp.maximum(best, peaks_z[k - 1, 0:1, :])
    put_peak(3, best)
    send(peak.at[3, one_row], peaks_end.at[one_row], other_core).wait_recv()
    amax = jnp.max(jnp.maximum(best, peaks_end[0:1, :]), axis=1, keepdims=True)

    lane = lax.broadcasted_iota(jnp.int32, (1, 16), 1)
    new_history = jnp.where(lane == 0, amax, jnp.roll(hist_ref[...], 1, axis=1))
    hist_out[...] = new_history
    out_scale = LIMIT / jnp.max(new_history)
    wq_out[...] = (weight_sum * out_scale).reshape(16, 512)

    for copy in sent:
        copy.wait_send()

    @pl.when(even)
    def _():
        for copy in even_first() + even_then(2) + even_then(6):
            copy.wait_send()

    @pl.when(jnp.logical_not(even))
    def _():
        for copy in odd_then():
            copy.wait_send()

    put_ig.wait()


def write_out(ig_in, wq_in, hist_in, ig_out, wq_out, hist_out):
    ig_out[...] = ig_in[...]
    wq_out[...] = wq_in[...].astype(BF16)
    hist_out[...] = hist_in[...]


def shards(out_grad, saved_input, weight, amax_history):
    any_space = pl.BlockSpec(memory_space=pl.ANY)
    vmem = pl.BlockSpec(memory_space=pltpu.VMEM)
    part = (8, 512)
    input_grad, weight_q, history = pl.pallas_call(
        kernel,
        out_shape=(
            jax.ShapeDtypeStruct((192, 512), BF16),
            jax.ShapeDtypeStruct((16, 512), F32),
            jax.ShapeDtypeStruct((1, 16), F32),
        ),
        in_specs=[any_space, any_space, any_space, vmem],
        out_specs=[any_space, vmem, vmem],
        scratch_shapes=[
            pltpu.VMEM((192, 4096), BF16),
            pltpu.VMEM((192, 512), BF16),
            pltpu.VMEM((512, 4096), BF16),
            pltpu.VMEM((192, 512), BF16),
            pltpu.VMEM((192, 512), F32),
            pltpu.VMEM((4, 192, 512), F32),
            pltpu.VMEM((192, 512), F32),
            pltpu.VMEM((4, 192, 512), F32),
            pltpu.VMEM((192, 512), BF16),
            pltpu.VMEM((2, 4, 4, 4, 2) + part, F32),
            pltpu.VMEM((2, 2, 2, 4, 2) + part, F32),
            pltpu.VMEM((2, 2, 4, 4, 2) + part, F32),
            pltpu.VMEM((2, 2, 2, 2) + part, F32),
            pltpu.VMEM((2, 2, 4, 2) + part, F32),
            pltpu.VMEM((4, 2, 2) + part, F32),
            pltpu.VMEM((2, 2, 2) + part, F32),
            pltpu.VMEM((2, 2) + part, F32),
            pltpu.VMEM((NB, 2) + part, F32),
            pltpu.VMEM((2 * NX * NY, 8, 128), F32),
            pltpu.VMEM((NZ // 2, 8, 128), F32),
            pltpu.VMEM((8, 128), F32),
            pltpu.VMEM((4, 8, 128), F32),
            pltpu.SemaphoreType.DMA((7,)),
            pltpu.SemaphoreType.DMA((N_SENT,)),
            pltpu.SemaphoreType.DMA((N_SENT,)),
            pltpu.SemaphoreType.DMA((9,)),
            pltpu.SemaphoreType.DMA((NB,)),
            pltpu.SemaphoreType.DMA((4,)),
            pltpu.SemaphoreType.REGULAR((4,)),
        ],
        compiler_params=pltpu.CompilerParams(
            collective_id=0, has_side_effects=True, vmem_limit_bytes=60 * 2**20
        ),
        name="all_steps",
    )(out_grad, saved_input, weight, amax_history.reshape(1, 16))
    input_grad, weight_q, history = pl.pallas_call(
        write_out,
        out_shape=(
            jax.ShapeDtypeStruct((192, 512), BF16),
            jax.ShapeDtypeStruct((16, 512), BF16),
            jax.ShapeDtypeStruct((1, 16), F32),
        ),
        in_specs=[vmem, vmem, vmem],
        out_specs=[vmem, vmem, vmem],
        compiler_params=pltpu.CompilerParams(vmem_limit_bytes=60 * 2**20),
        name="write_out",
    )(input_grad, weight_q, history)
    return (input_grad, weight_q.T, history.reshape(16))


def solution(mesh):
    placed = (P("dp", None), P("dp", "tensor"), P("tensor", None), P())
    return jax.shard_map(
        shards,
        mesh=mesh,
        in_specs=placed,
        out_specs=(P("dp", "tensor"), P("tensor", "dp"), P()),
        check_vma=False,
    )
```

```python
import jax
import jax.numpy as jnp
from jax import lax
from jax.experimental import pallas as pl
from jax.experimental.pallas import tpu as pltpu
from jax.sharding import PartitionSpec as P

LIMIT = 8.0
MESH = pl.DeviceIdType.MESH
NX, NZ, NY = 4, 32, 4
NB = NZ // 4
F32, BF16 = jnp.float32, jnp.bfloat16
ORDER = (2, 1, 3, 0)
PLACE = {k: n for n, k in enumerate(ORDER)}
N_SENT = 5 + 12 + 12 + (2 * NX * NY - 1) + (NZ - 1)


def kernel(
    og_hbm, si_hbm, w_hbm, hist_ref,
    ig_out, wq_out, hist_out,
    og, si, w, ig, si_sent, og_sent, si_core, og_core, si_other,
    terms, pass_one, in_one, pass_two, in_two, ready, relay, relay_far, in_last,
    peaks_plane, peaks_z, peak,
    local_sem, send_sem, recv_sem, last_send, last_recv, relay_sem, hello,
):
    dp, y = lax.axis_index("dp"), lax.axis_index("tensor")
    x, z, c = dp // (2 * NZ), lax.rem(dp // 2, NZ), lax.rem(dp, 2)
    zc, zb = lax.rem(z, 4), z // 4

    def device(x, y, z, c):
        return ((x * NZ + z) * 2 + c, y)

    def along_x(d):
        return device(lax.rem(x + d + NX, NX), y, z, c)

    def along_y(d):
        return device(x, lax.rem(y + d + NY, NY), z, c)

    def along_z(d, core=None):
        return device(x, y, lax.rem(z + d + NZ, NZ), c if core is None else core)

    def in_plane(dx, dy, dc):
        return device(lax.rem(x + dx, NX), lax.rem(y + dy, NY), z, lax.rem(c + dc, 2))

    other_core = device(x, y, z, 1 - c)
    sides = [along_x(1), along_x(-1), along_y(1), along_y(-1)]

    def signal(sem, devices):
        for to in devices:
            pl.semaphore_signal(sem, inc=1, device_id=to, device_id_type=MESH)

    barrier = pltpu.get_barrier_semaphore()
    near = [other_core, along_z(1), along_z(-1)] + sides
    signal(barrier, near)
    rounds = [
        sides + [along_z(1), along_z(-1)],
        sides + [along_z(2), along_z(-2)],
        sides + [along_z(4), along_z(-4)],
        [along_z(8), along_z(-8)],
    ]

    def say(n):
        signal(hello.at[n], rounds[n])

    def hear(n):
        pl.semaphore_wait(hello.at[n], len(rounds[n]))

    def columns_of(k):
        return pl.ds(pl.multiple_of(lax.rem(x + k, 4) * 1024, 1024), 1024)

    get_si = pltpu.make_async_copy(si_hbm, si, local_sem.at[0])
    get_og = [
        pltpu.make_async_copy(
            og_hbm.at[:, columns_of(k)], og.at[:, columns_of(k)], local_sem.at[1 + n]
        )
        for n, k in enumerate(ORDER)
    ]
    get_w = pltpu.make_async_copy(w_hbm, w, local_sem.at[5])
    get_si.start()
    for copy in get_og:
        copy.start()

    used = [0]
    sent = []

    def send(src, dst, to):
        n = used[0]
        used[0] += 1
        copy = pltpu.make_async_remote_copy(
            src_ref=src, dst_ref=dst, send_sem=send_sem.at[n], recv_sem=recv_sem.at[n],
            device_id=to, device_id_type=MESH,
        )
        copy.start()
        sent.append(copy)
        return copy

    scale_in = LIMIT / jnp.max(hist_ref[...])

    def group(at, i, core):
        return pl.ds(pl.multiple_of(at * 1024 + i * 256 + core * 128, 128), 128)

    get_si.wait()
    si_sent[...] = si[...].astype(F32)
    og_copies = []
    for n, k in enumerate(ORDER):
        get_og[n].wait()
        for i in range(4):
            og_sent[n, :, i * 128 : i * 128 + 128] = og[
                :, group(lax.rem(x + k, 4), i, 1 - c)
            ].astype(F32)
        if n == 0:
            pl.semaphore_wait(barrier, len(near))
            si_copy = send(si_sent, si_core, other_core)
        og_copies.append(send(og_sent.at[n], og_core.at[n], other_core))
    get_w.start()
    say(0)

    def quantized(grads, inputs):
        term = lax.dot_general(
            grads, inputs, (((0,), (0,)), ((), ())), preferred_element_type=F32
        )
        return jnp.clip(term * scale_in, -LIMIT, LIMIT).astype(BF16).astype(F32)

    def pieces(at, n, first):
        for i in range(2):
            for j in range(4):
                for core in range(2):
                    row = i * 128 + j * 32 + core * 16
                    yield (0, at, j, first + i, core), row
                    yield (1, j, n, first + i, core), row + 8

    def own_tile(n, k):
        at = lax.rem(x + k, 4)

        @pl.loop(0, 2)
        def _(s):
            grads = jnp.concatenate(
                [og[:, group(at, 2 * s, c)], og[:, group(at, 2 * s + 1, c)]], axis=1
            )
            quant = quantized(grads, si[...])
            for where, row in pieces(at, n, 2 * s):
                terms[where] = quant[row : row + 8]

    def other_tile(n, k):
        at = lax.rem(x + k, 4)
        if n == 0:
            si_copy.wait_recv()
            si_other[...] = si_core[...].astype(BF16)
        og_copies[n].wait_recv()

        @pl.loop(0, 2)
        def _(s):
            columns = pl.ds(pl.multiple_of(s * 256, 256), 256)
            quant = quantized(og_core[n, :, columns].astype(BF16), si_other[...])
            for where, row in pieces(at, n, 2 * s):
                terms[where] += quant[row : row + 8]

    A, B = pl.ds(0, 2), pl.ds(2, 2)
    plus = (along_x(1), along_z(1))
    minus = (along_x(-1), along_z(-1))
    first = (x, zc)

    def unit(p, k):
        return terms.at[p, lax.rem(first[p] + k, 4)]

    one = [{}, {}]
    own_tile(0, 2)
    other_tile(0, 2)
    one[0]["a+"] = send(unit(0, 2).at[A], pass_one.at[0, 0], plus[0])
    one[0]["a-"] = send(unit(0, 2).at[B], pass_one.at[0, 1], minus[0])
    hear(0)
    say(1)
    own_tile(1, 1)
    other_tile(1, 1)
    one[1]["a+"] = send(unit(1, 2).at[A], pass_one.at[1, 0], plus[1])
    one[0]["b+"] = send(unit(0, 1).at[B], in_one.at[0, 0, B], plus[0])
    one[1]["b-"] = send(unit(1, 3).at[A], in_one.at[1, 1, A], minus[1])
    own_tile(2, 3)
    other_tile(2, 3)
    one[0]["b-"] = send(unit(0, 3).at[A], in_one.at[0, 1, A], minus[0])
    own_tile(3, 0)
    other_tile(3, 0)
    one[1]["a-"] = send(unit(1, 2).at[B], pass_one.at[1, 1], minus[1])
    one[1]["b+"] = send(unit(1, 1).at[B], in_one.at[1, 0, B], plus[1])
    hear(1)
    say(2)

    def pass_on(p, k, half, at, key_in, key_out, to):
        one[p][key_in].wait_recv()
        m = lax.rem(first[p] + k, 4)
        terms[p, m, half] += pass_one[p, at]
        one[p][key_out] = send(terms.at[p, m, half], in_one.at[p, at, half], to)

    pass_on(0, 1, A, 0, "a+", "c+", plus[0])
    pass_on(0, 3, B, 1, "a-", "c-", minus[0])
    pass_on(1, 1, A, 0, "a+", "c+", plus[1])
    pass_on(1, 3, B, 1, "a-", "c-", minus[1])

    get_w.wait()

    @pl.loop(0, 2)
    def _(i):
        rows = pl.ds(pl.multiple_of(i * 256, 256), 256)
        ig[:, rows] = lax.dot_general(
            og[...], w[rows, :], (((1,), (1,)), ((), ())), preferred_element_type=F32
        ).astype(BF16)

    put_ig = pltpu.make_async_copy(ig, ig_out, local_sem.at[6])
    put_ig.start()
    hear(2)
    say(3)

    C, D = pl.ds(0, 2), pl.ds(2, 2)
    two = [{}, {}]
    up, down = (plus[1], plus[0]), (minus[1], minus[0])

    def second(p, k):
        return lax.rem(zc + k, 4) if p == 0 else PLACE[k]

    def second_start(p):
        for key in ("b+", "b-", "c+", "c-"):
            one[p][key].wait_recv()
        m = first[p]

        def total(k):
            q = second(p, k)
            terms[p, m, q] += in_one[p, 0, q] + in_one[p, 1, q]
            return terms.at[p, m, q]

        far = total(2)
        two[p]["a+"] = send(far.at[C], pass_two.at[p, 0], up[p])
        two[p]["a-"] = send(far.at[D], pass_two.at[p, 1], down[p])
        two[p]["b+"] = send(total(1).at[D], in_two.at[p, 0, D], up[p])
        two[p]["b-"] = send(total(3).at[C], in_two.at[p, 1, C], down[p])
        total(0)

    def second_pass(p):
        m = first[p]
        for key, out, k, half, at, to in (
            ("a+", "c+", 1, C, 0, up[p]),
            ("a-", "c-", 3, D, 1, down[p]),
        ):
            q = second(p, k)
            two[p][key].wait_recv()
            terms[p, m, q, half] += pass_two[p, at]
            two[p][out] = send(terms.at[p, m, q, half], in_two.at[p, at, half], to)

    def second_end(p):
        for key in ("b+", "b-", "c+", "c-"):
            two[p][key].wait_recv()
        ready[:, p] = terms[p, first[p], second(p, 0)] + in_two[p, 0] + in_two[p, 1]

    even = lax.rem(zb, 2) == c
    odd = jnp.logical_not(even)

    def block(k):
        return lax.rem(zb + k, NB) // 2

    def last_copy(n, src, dst, recv, to):
        return pltpu.make_async_remote_copy(
            src_ref=src, dst_ref=dst, send_sem=last_send.at[n], recv_sem=recv,
            device_id=to, device_id_type=MESH,
        )

    def piece(n, k, p, core):
        return last_copy(
            n, ready.at[block(k), p, core], in_last.at[k, p], last_recv.at[2 * k + p],
            along_z(4 * k, core),
        )

    def to_core(n, p):
        return last_copy(
            n, ready.at[block(0), p, 1 - c], in_last.at[0, p], last_recv.at[p], other_core
        )

    def relay_half(n, p, at):
        return last_copy(
            n, ready.at[block(4), p, at], relay_far.at[p, at], relay_sem.at[2 * p + at],
            along_z(8 if at == 0 else -8),
        )

    def relay_whole(n, p, at):
        return last_copy(
            n, ready.at[block(3 if at == 0 else 5), p], relay.at[p, at],
            relay_sem.at[4 + 2 * p + at], along_z(4 if at == 0 else -4),
        )

    def even_first(p):
        return [relay_half(8 * p, p, 0), relay_half(8 * p + 1, p, 1), to_core(8 * p + 2, p)]

    def even_then(p, k):
        n = 8 * p + (3 if k == 2 else 5)
        return [piece(n, k, p, 0), piece(n + 1, k, p, 1)]

    def odd_copies(p):
        n = 8 * p
        return [
            relay_whole(n, p, 0), relay_whole(n + 1, p, 1), piece(n + 2, 1, p, 0),
            piece(n + 3, 7, p, 0), piece(n + 4, 1, p, 1), piece(n + 5, 7, p, 1),
        ]

    def last_start(p):
        @pl.when(even)
        def _():
            for copy in even_first(p):
                copy.start()
            in_last[0, p] = ready[zb // 2, p, c]

        @pl.when(odd)
        def _():
            for copy in odd_copies(p):
                copy.start()

    def last_pass(p):
        @pl.when(even)
        def _():
            for at, k in ((0, 2), (1, 6)):
                relay_whole(0, p, at).wait_recv()
                ready[block(k), p] += relay[p, at]
                relay_half(0, p, at).wait_recv()
                ready[block(k), p, at] += relay_far[p, at]
                for copy in even_then(p, k):
                    copy.start()

        @pl.when(odd)
        def _():
            last_copy(
                0, in_last.at[0, p], in_last.at[0, p], last_recv.at[p], other_core
            ).wait_recv()

    second_start(0)
    second_pass(0)
    second_start(1)
    second_end(0)
    hear(3)
    last_start(0)
    second_pass(1)
    second_end(1)
    last_start(1)
    for p in range(2):
        last_pass(p)
    for p in range(2):
        for k in (1, 7, 2, 6):
            piece(0, k, p, 0).wait_recv()
    summed = in_last[0]
    for k in (1, 7, 2, 6):
        summed = summed + in_last[k]
    weight_sum = summed / scale_in

    one_row = pl.ds(0, 1)

    def largest(best, at, slots, devices):
        peak[at, 0:1, :] = best
        copies = [
            (d, send(peak.at[at, one_row], slots.at[d, one_row], to)) for d, to in devices
        ]
        for d, copy in copies:
            copy.wait_recv()
            best = jnp.maximum(best, slots[d, 0:1, :])
        return best

    def way(d, n):
        return min(d, n - d)

    plane = sorted(
        range(1, 2 * NX * NY), key=lambda d: -way(d // 2 // NY, NX) - way(d // 2 % NY, NY)
    )
    line = sorted(range(1, NZ), key=lambda d: -way(d, NZ))
    top = jnp.max(jnp.max(jnp.abs(weight_sum), axis=0), axis=0, keepdims=True)
    best = top[:, 0:128]
    for i in range(1, 4):
        best = jnp.maximum(best, top[:, i * 128 : i * 128 + 128])
    best = largest(
        best, 0, peaks_plane, [(d, in_plane(d // 2 // NY, d // 2 % NY, d % 2)) for d in plane]
    )
    best = largest(best, 1, peaks_z, [(d, along_z(d)) for d in line])
    amax = jnp.max(best, axis=1, keepdims=True)

    lane = lax.broadcasted_iota(jnp.int32, (1, 16), 1)
    new_history = jnp.where(lane == 0, amax, jnp.roll(hist_ref[...], 1, axis=1))
    hist_out[...] = new_history
    out_scale = LIMIT / jnp.max(new_history)
    wq_out[...] = (weight_sum * out_scale).reshape(16, 512)

    for copy in sent:
        copy.wait_send()

    @pl.when(even)
    def _():
        for p in range(2):
            for copy in even_first(p) + even_then(p, 2) + even_then(p, 6):
                copy.wait_send()

    @pl.when(odd)
    def _():
        for p in range(2):
            for copy in odd_copies(p):
                copy.wait_send()

    put_ig.wait()


def write_out(ig_in, wq_in, hist_in, ig_out, wq_out, hist_out):
    ig_out[...] = ig_in[...]
    wq_out[...] = wq_in[...].astype(BF16)
    hist_out[...] = hist_in[...]


def shards(out_grad, saved_input, weight, amax_history):
    any_space = pl.BlockSpec(memory_space=pl.ANY)
    vmem = pl.BlockSpec(memory_space=pltpu.VMEM)
    part = (8, 512)
    input_grad, weight_q, history = pl.pallas_call(
        kernel,
        out_shape=(
            jax.ShapeDtypeStruct((192, 512), BF16),
            jax.ShapeDtypeStruct((16, 512), F32),
            jax.ShapeDtypeStruct((1, 16), F32),
        ),
        in_specs=[any_space, any_space, any_space, vmem],
        out_specs=[any_space, vmem, vmem],
        scratch_shapes=[
            pltpu.VMEM((192, 4096), BF16),
            pltpu.VMEM((192, 512), BF16),
            pltpu.VMEM((512, 4096), BF16),
            pltpu.VMEM((192, 512), BF16),
            pltpu.VMEM((192, 512), F32),
            pltpu.VMEM((4, 192, 512), F32),
            pltpu.VMEM((192, 512), F32),
            pltpu.VMEM((4, 192, 512), F32),
            pltpu.VMEM((192, 512), BF16),
            pltpu.VMEM((2, 4, 4, 4, 2) + part, F32),
            pltpu.VMEM((2, 2, 2, 4, 2) + part, F32),
            pltpu.VMEM((2, 2, 4, 4, 2) + part, F32),
            pltpu.VMEM((2, 2, 2, 2) + part, F32),
            pltpu.VMEM((2, 2, 4, 2) + part, F32),
            pltpu.VMEM((4, 2, 2) + part, F32),
            pltpu.VMEM((2, 2, 2) + part, F32),
            pltpu.VMEM((2, 2) + part, F32),
            pltpu.VMEM((NB, 2) + part, F32),
            pltpu.VMEM((2 * NX * NY, 8, 128), F32),
            pltpu.VMEM((NZ, 8, 128), F32),
            pltpu.VMEM((2, 8, 128), F32),
            pltpu.SemaphoreType.DMA((7,)),
            pltpu.SemaphoreType.DMA((N_SENT,)),
            pltpu.SemaphoreType.DMA((N_SENT,)),
            pltpu.SemaphoreType.DMA((16,)),
            pltpu.SemaphoreType.DMA((2 * NB,)),
            pltpu.SemaphoreType.DMA((8,)),
            pltpu.SemaphoreType.REGULAR((4,)),
        ],
        compiler_params=pltpu.CompilerParams(
            collective_id=0, has_side_effects=True, vmem_limit_bytes=60 * 2**20
        ),
        name="all_steps",
    )(out_grad, saved_input, weight, amax_history.reshape(1, 16))
    input_grad, weight_q, history = pl.pallas_call(
        write_out,
        out_shape=(
            jax.ShapeDtypeStruct((192, 512), BF16),
            jax.ShapeDtypeStruct((16, 512), BF16),
            jax.ShapeDtypeStruct((1, 16), F32),
        ),
        in_specs=[vmem, vmem, vmem],
        out_specs=[vmem, vmem, vmem],
        compiler_params=pltpu.CompilerParams(vmem_limit_bytes=60 * 2**20),
        name="write_out",
    )(input_grad, weight_q, history)
    return (input_grad, weight_q.T, history.reshape(16))


def solution(mesh):
    placed = (P("dp", None), P("dp", "tensor"), P("tensor", None), P())
    return jax.shard_map(
        shards,
        mesh=mesh,
        in_specs=placed,
        out_specs=(P("dp", "tensor"), P("tensor", "dp"), P()),
        check_vma=False,
    )
```

```python
import jax
import jax.numpy as jnp
from jax import lax
from jax.experimental import pallas as pl
from jax.experimental.pallas import tpu as pltpu
from jax.sharding import PartitionSpec as P

LIMIT = 8.0
MESH = pl.DeviceIdType.MESH
NX, NZ, NY = 4, 32, 4
NB = NZ // 4
F32, BF16 = jnp.float32, jnp.bfloat16
ORDER = (2, 1, 3, 0)
PLACE = {k: n for n, k in enumerate(ORDER)}
N_SENT = 5 + 12 + 12 + (2 * NX * NY - 1) + (NZ - 1)


def kernel(
    og_hbm, si_hbm, w_hbm, hist_hbm,
    ig_out, wq_out, hist_out,
    hist_ref, og, si, w, ig, si_sent, og_sent, si_core, og_core, si_other,
    terms, pass_one, in_one, pass_two, in_two, ready, relay, relay_far, in_last,
    peaks_plane, peaks_z, peak,
    local_sem, send_sem, recv_sem, last_send, last_recv, relay_sem, hello,
):
    dp, y = lax.axis_index("dp"), lax.axis_index("tensor")
    x, z, c = dp // (2 * NZ), lax.rem(dp // 2, NZ), lax.rem(dp, 2)
    zc, zb = lax.rem(z, 4), z // 4

    def device(x, y, z, c):
        return ((x * NZ + z) * 2 + c, y)

    def along_x(d):
        return device(lax.rem(x + d + NX, NX), y, z, c)

    def along_y(d):
        return device(x, lax.rem(y + d + NY, NY), z, c)

    def along_z(d, core=None):
        return device(x, y, lax.rem(z + d + NZ, NZ), c if core is None else core)

    def in_plane(dx, dy, dc):
        return device(lax.rem(x + dx, NX), lax.rem(y + dy, NY), z, lax.rem(c + dc, 2))

    other_core = device(x, y, z, 1 - c)
    sides = [along_x(1), along_x(-1), along_y(1), along_y(-1)]

    def signal(sem, devices):
        for to in devices:
            pl.semaphore_signal(sem, inc=1, device_id=to, device_id_type=MESH)

    barrier = pltpu.get_barrier_semaphore()
    near = [other_core, along_z(1), along_z(-1)] + sides
    signal(barrier, near)
    rounds = [
        sides + [along_z(1), along_z(-1)],
        sides + [along_z(2), along_z(-2)],
        sides + [along_z(4), along_z(-4)],
        [along_z(8), along_z(-8)],
    ]

    def say(n):
        signal(hello.at[n], rounds[n])

    def hear(n):
        pl.semaphore_wait(hello.at[n], len(rounds[n]))

    def columns_of(k):
        return pl.ds(pl.multiple_of(lax.rem(x + k, 4) * 1024, 1024), 1024)

    get_si = pltpu.make_async_copy(si_hbm, si, local_sem.at[0])
    get_og = [
        pltpu.make_async_copy(
            og_hbm.at[:, columns_of(k)], og.at[:, columns_of(k)], local_sem.at[1 + n]
        )
        for n, k in enumerate(ORDER)
    ]
    get_w = pltpu.make_async_copy(w_hbm, w, local_sem.at[5])
    get_hist = pltpu.make_async_copy(hist_hbm, hist_ref, local_sem.at[7])
    get_si.start()
    for copy in get_og:
        copy.start()
    get_hist.start()

    used = [0]
    sent = []

    def send(src, dst, to):
        n = used[0]
        used[0] += 1
        copy = pltpu.make_async_remote_copy(
            src_ref=src, dst_ref=dst, send_sem=send_sem.at[n], recv_sem=recv_sem.at[n],
            device_id=to, device_id_type=MESH,
        )
        copy.start()
        sent.append(copy)
        return copy


    def group(at, i, core):
        return pl.ds(pl.multiple_of(at * 1024 + i * 256 + core * 128, 128), 128)

    get_si.wait()
    si_sent[...] = si[...].astype(F32)
    og_copies = []
    for n, k in enumerate(ORDER):
        get_og[n].wait()
        for i in range(4):
            og_sent[n, :, i * 128 : i * 128 + 128] = og[
                :, group(lax.rem(x + k, 4), i, 1 - c)
            ].astype(F32)
        if n == 0:
            pl.semaphore_wait(barrier, len(near))
            si_copy = send(si_sent, si_core, other_core)
        og_copies.append(send(og_sent.at[n], og_core.at[n], other_core))
    get_w.start()
    say(0)
    get_hist.wait()
    scale_in = LIMIT / jnp.max(hist_ref[...])

    def quantized(grads, inputs):
        term = lax.dot_general(
            grads, inputs, (((0,), (0,)), ((), ())), preferred_element_type=F32
        )
        return jnp.clip(term * scale_in, -LIMIT, LIMIT).astype(BF16).astype(F32)

    def pieces(at, n, first):
        for i in range(2):
            for j in range(4):
                for core in range(2):
                    row = i * 128 + j * 32 + core * 16
                    yield (0, at, j, first + i, core), row
                    yield (1, j, n, first + i, core), row + 8

    def own_tile(n, k):
        at = lax.rem(x + k, 4)

        @pl.loop(0, 2)
        def _(s):
            grads = jnp.concatenate(
                [og[:, group(at, 2 * s, c)], og[:, group(at, 2 * s + 1, c)]], axis=1
            )
            quant = quantized(grads, si[...])
            for where, row in pieces(at, n, 2 * s):
                terms[where] = quant[row : row + 8]

    def other_tile(n, k):
        at = lax.rem(x + k, 4)
        if n == 0:
            si_copy.wait_recv()
            si_other[...] = si_core[...].astype(BF16)
        og_copies[n].wait_recv()

        @pl.loop(0, 2)
        def _(s):
            columns = pl.ds(pl.multiple_of(s * 256, 256), 256)
            quant = quantized(og_core[n, :, columns].astype(BF16), si_other[...])
            for where, row in pieces(at, n, 2 * s):
                terms[where] += quant[row : row + 8]

    A, B = pl.ds(0, 2), pl.ds(2, 2)
    plus = (along_x(1), along_z(1))
    minus = (along_x(-1), along_z(-1))
    first = (x, zc)

    def unit(p, k):
        return terms.at[p, lax.rem(first[p] + k, 4)]

    one = [{}, {}]
    own_tile(0, 2)
    other_tile(0, 2)
    one[0]["a+"] = send(unit(0, 2).at[A], pass_one.at[0, 0], plus[0])
    one[0]["a-"] = send(unit(0, 2).at[B], pass_one.at[0, 1], minus[0])
    hear(0)
    say(1)
    own_tile(1, 1)
    other_tile(1, 1)
    one[1]["a+"] = send(unit(1, 2).at[A], pass_one.at[1, 0], plus[1])
    one[0]["b+"] = send(unit(0, 1).at[B], in_one.at[0, 0, B], plus[0])
    one[1]["b-"] = send(unit(1, 3).at[A], in_one.at[1, 1, A], minus[1])
    own_tile(2, 3)
    other_tile(2, 3)
    one[0]["b-"] = send(unit(0, 3).at[A], in_one.at[0, 1, A], minus[0])
    own_tile(3, 0)
    other_tile(3, 0)
    one[1]["a-"] = send(unit(1, 2).at[B], pass_one.at[1, 1], minus[1])
    one[1]["b+"] = send(unit(1, 1).at[B], in_one.at[1, 0, B], plus[1])
    hear(1)
    say(2)

    def pass_on(p, k, half, at, key_in, key_out, to):
        one[p][key_in].wait_recv()
        m = lax.rem(first[p] + k, 4)
        terms[p, m, half] += pass_one[p, at]
        one[p][key_out] = send(terms.at[p, m, half], in_one.at[p, at, half], to)

    pass_on(0, 1, A, 0, "a+", "c+", plus[0])
    pass_on(0, 3, B, 1, "a-", "c-", minus[0])
    pass_on(1, 1, A, 0, "a+", "c+", plus[1])
    pass_on(1, 3, B, 1, "a-", "c-", minus[1])

    get_w.wait()

    @pl.loop(0, 2)
    def _(i):
        rows = pl.ds(pl.multiple_of(i * 256, 256), 256)
        ig[:, rows] = lax.dot_general(
            og[...], w[rows, :], (((1,), (1,)), ((), ())), preferred_element_type=F32
        ).astype(BF16)

    put_ig = pltpu.make_async_copy(ig, ig_out, local_sem.at[6])
    put_ig.start()
    hear(2)
    say(3)

    C, D = pl.ds(0, 2), pl.ds(2, 2)
    two = [{}, {}]
    up, down = (plus[1], plus[0]), (minus[1], minus[0])

    def second(p, k):
        return lax.rem(zc + k, 4) if p == 0 else PLACE[k]

    def second_start(p):
        for key in ("b+", "b-", "c+", "c-"):
            one[p][key].wait_recv()
        m = first[p]

        def total(k):
            q = second(p, k)
            terms[p, m, q] += in_one[p, 0, q] + in_one[p, 1, q]
            return terms.at[p, m, q]

        far = total(2)
        two[p]["a+"] = send(far.at[C], pass_two.at[p, 0], up[p])
        two[p]["a-"] = send(far.at[D], pass_two.at[p, 1], down[p])
        two[p]["b+"] = send(total(1).at[D], in_two.at[p, 0, D], up[p])
        two[p]["b-"] = send(total(3).at[C], in_two.at[p, 1, C], down[p])
        total(0)

    def second_pass(p):
        m = first[p]
        for key, out, k, half, at, to in (
            ("a+", "c+", 1, C, 0, up[p]),
            ("a-", "c-", 3, D, 1, down[p]),
        ):
            q = second(p, k)
            two[p][key].wait_recv()
            terms[p, m, q, half] += pass_two[p, at]
            two[p][out] = send(terms.at[p, m, q, half], in_two.at[p, at, half], to)

    def second_end(p):
        for key in ("b+", "b-", "c+", "c-"):
            two[p][key].wait_recv()
        ready[:, p] = terms[p, first[p], second(p, 0)] + in_two[p, 0] + in_two[p, 1]

    even = lax.rem(zb, 2) == c
    odd = jnp.logical_not(even)

    def block(k):
        return lax.rem(zb + k, NB) // 2

    def last_copy(n, src, dst, recv, to):
        return pltpu.make_async_remote_copy(
            src_ref=src, dst_ref=dst, send_sem=last_send.at[n], recv_sem=recv,
            device_id=to, device_id_type=MESH,
        )

    def piece(n, k, p, core):
        return last_copy(
            n, ready.at[block(k), p, core], in_last.at[k, p], last_recv.at[2 * k + p],
            along_z(4 * k, core),
        )

    def to_core(n, p):
        return last_copy(
            n, ready.at[block(0), p, 1 - c], in_last.at[0, p], last_recv.at[p], other_core
        )

    def relay_half(n, p, at):
        return last_copy(
            n, ready.at[block(4), p, at], relay_far.at[p, at], relay_sem.at[2 * p + at],
            along_z(8 if at == 0 else -8),
        )

    def relay_whole(n, p, at):
        return last_copy(
            n, ready.at[block(3 if at == 0 else 5), p], relay.at[p, at],
            relay_sem.at[4 + 2 * p + at], along_z(4 if at == 0 else -4),
        )

    def even_first(p):
        return [relay_half(8 * p, p, 0), relay_half(8 * p + 1, p, 1), to_core(8 * p + 2, p)]

    def even_then(p, k):
        n = 8 * p + (3 if k == 2 else 5)
        return [piece(n, k, p, 0), piece(n + 1, k, p, 1)]

    def odd_copies(p):
        n = 8 * p
        return [
            relay_whole(n, p, 0), relay_whole(n + 1, p, 1), piece(n + 2, 1, p, 0),
            piece(n + 3, 7, p, 0), piece(n + 4, 1, p, 1), piece(n + 5, 7, p, 1),
        ]

    def last_start(p):
        @pl.when(even)
        def _():
            for copy in even_first(p):
                copy.start()
            in_last[0, p] = ready[zb // 2, p, c]

        @pl.when(odd)
        def _():
            for copy in odd_copies(p):
                copy.start()

    def last_pass(p):
        @pl.when(even)
        def _():
            for at, k in ((0, 2), (1, 6)):
                relay_whole(0, p, at).wait_recv()
                ready[block(k), p] += relay[p, at]
                relay_half(0, p, at).wait_recv()
                ready[block(k), p, at] += relay_far[p, at]
                for copy in even_then(p, k):
                    copy.start()

        @pl.when(odd)
        def _():
            last_copy(
                0, in_last.at[0, p], in_last.at[0, p], last_recv.at[p], other_core
            ).wait_recv()

    second_start(0)
    second_start(1)
    second_pass(0)
    second_pass(1)
    second_end(0)
    hear(3)
    last_start(0)
    second_end(1)
    last_start(1)
    for p in range(2):
        last_pass(p)
    for p in range(2):
        for k in (1, 7, 2, 6):
            piece(0, k, p, 0).wait_recv()
    summed = in_last[0]
    for k in (1, 7, 2, 6):
        summed = summed + in_last[k]
    weight_sum = summed / scale_in

    one_row = pl.ds(0, 1)

    def largest(best, at, slots, devices):
        peak[at, 0:1, :] = best
        copies = [
            (d, send(peak.at[at, one_row], slots.at[d, one_row], to)) for d, to in devices
        ]
        for d, copy in copies:
            copy.wait_recv()
            best = jnp.maximum(best, slots[d, 0:1, :])
        return best

    def way(d, n):
        return min(d, n - d)

    plane = sorted(
        range(1, 2 * NX * NY), key=lambda d: -way(d // 2 // NY, NX) - way(d // 2 % NY, NY)
    )
    line = sorted(range(1, NZ), key=lambda d: -way(d, NZ))
    top = jnp.max(jnp.max(jnp.abs(weight_sum), axis=0), axis=0, keepdims=True)
    best = top[:, 0:128]
    for i in range(1, 4):
        best = jnp.maximum(best, top[:, i * 128 : i * 128 + 128])
    best = largest(
        best, 0, peaks_plane, [(d, in_plane(d // 2 // NY, d // 2 % NY, d % 2)) for d in plane]
    )
    best = largest(best, 1, peaks_z, [(d, along_z(d)) for d in line])
    amax = jnp.max(best, axis=1, keepdims=True)

    lane = lax.broadcasted_iota(jnp.int32, (1, 16), 1)
    new_history = jnp.where(lane == 0, amax, jnp.roll(hist_ref[...], 1, axis=1))
    hist_out[...] = new_history
    out_scale = LIMIT / jnp.max(new_history)
    wq_out[...] = (weight_sum * out_scale).reshape(16, 512)

    for copy in sent:
        copy.wait_send()

    @pl.when(even)
    def _():
        for p in range(2):
            for copy in even_first(p) + even_then(p, 2) + even_then(p, 6):
                copy.wait_send()

    @pl.when(odd)
    def _():
        for p in range(2):
            for copy in odd_copies(p):
                copy.wait_send()

    put_ig.wait()


def write_out(ig_in, wq_in, hist_in, ig_out, wq_out, hist_out):
    ig_out[...] = ig_in[...]
    wq_out[...] = wq_in[...].astype(BF16)
    hist_out[...] = hist_in[...]


def shards(out_grad, saved_input, weight, amax_history):
    any_space = pl.BlockSpec(memory_space=pl.ANY)
    vmem = pl.BlockSpec(memory_space=pltpu.VMEM)
    part = (8, 512)
    input_grad, weight_q, history = pl.pallas_call(
        kernel,
        out_shape=(
            jax.ShapeDtypeStruct((192, 512), BF16),
            jax.ShapeDtypeStruct((16, 512), F32),
            jax.ShapeDtypeStruct((1, 16), F32),
        ),
        in_specs=[any_space] * 4,
        out_specs=[any_space, vmem, vmem],
        scratch_shapes=[
            pltpu.VMEM((1, 16), F32),
            pltpu.VMEM((192, 4096), BF16),
            pltpu.VMEM((192, 512), BF16),
            pltpu.VMEM((512, 4096), BF16),
            pltpu.VMEM((192, 512), BF16),
            pltpu.VMEM((192, 512), F32),
            pltpu.VMEM((4, 192, 512), F32),
            pltpu.VMEM((192, 512), F32),
            pltpu.VMEM((4, 192, 512), F32),
            pltpu.VMEM((192, 512), BF16),
            pltpu.VMEM((2, 4, 4, 4, 2) + part, F32),
            pltpu.VMEM((2, 2, 2, 4, 2) + part, F32),
            pltpu.VMEM((2, 2, 4, 4, 2) + part, F32),
            pltpu.VMEM((2, 2, 2, 2) + part, F32),
            pltpu.VMEM((2, 2, 4, 2) + part, F32),
            pltpu.VMEM((4, 2, 2) + part, F32),
            pltpu.VMEM((2, 2, 2) + part, F32),
            pltpu.VMEM((2, 2) + part, F32),
            pltpu.VMEM((NB, 2) + part, F32),
            pltpu.VMEM((2 * NX * NY, 8, 128), F32),
            pltpu.VMEM((NZ, 8, 128), F32),
            pltpu.VMEM((2, 8, 128), F32),
            pltpu.SemaphoreType.DMA((8,)),
            pltpu.SemaphoreType.DMA((N_SENT,)),
            pltpu.SemaphoreType.DMA((N_SENT,)),
            pltpu.SemaphoreType.DMA((16,)),
            pltpu.SemaphoreType.DMA((2 * NB,)),
            pltpu.SemaphoreType.DMA((8,)),
            pltpu.SemaphoreType.REGULAR((4,)),
        ],
        compiler_params=pltpu.CompilerParams(
            collective_id=0, has_side_effects=True, vmem_limit_bytes=60 * 2**20
        ),
        name="all_steps",
    )(out_grad, saved_input, weight, amax_history.reshape(1, 16))
    input_grad, weight_q, history = pl.pallas_call(
        write_out,
        out_shape=(
            jax.ShapeDtypeStruct((192, 512), BF16),
            jax.ShapeDtypeStruct((16, 512), BF16),
            jax.ShapeDtypeStruct((1, 16), F32),
        ),
        in_specs=[vmem, vmem, vmem],
        out_specs=[vmem, vmem, vmem],
        compiler_params=pltpu.CompilerParams(vmem_limit_bytes=60 * 2**20),
        name="write_out",
    )(input_grad, weight_q, history)
    return (input_grad, weight_q.T, history.reshape(16))


def solution(mesh):
    placed = (P("dp", None), P("dp", "tensor"), P("tensor", None), P())
    return jax.shard_map(
        shards,
        mesh=mesh,
        in_specs=placed,
        out_specs=(P("dp", "tensor"), P("tensor", "dp"), P()),
        check_vma=False,
    )
```

```python
import jax
import jax.numpy as jnp
from jax import lax
from jax.experimental import pallas as pl
from jax.experimental.pallas import tpu as pltpu
from jax.sharding import PartitionSpec as P

LIMIT = 8.0
MESH = pl.DeviceIdType.MESH
NX, NZ, NY = 4, 32, 4
NB = NZ // 4
F32, BF16 = jnp.float32, jnp.bfloat16
ORDER = (2, 1, 3, 0)
PLACE = {k: n for n, k in enumerate(ORDER)}
N_SENT = 5 + 12 + 12 + (NX * NY - 1) + (NZ - 1) + 1


def kernel(
    og_hbm, si_hbm, w_hbm, hist_hbm,
    ig_out, wq_out, hist_out,
    hist_ref, og, si, w, ig, si_sent, og_sent, si_core, og_core, si_other,
    terms, pass_one, in_one, pass_two, in_two, ready, relay, relay_far, in_last,
    peaks_plane, peaks_z, peak,
    local_sem, send_sem, recv_sem, last_send, last_recv, relay_sem, hello,
):
    dp, y = lax.axis_index("dp"), lax.axis_index("tensor")
    x, z, c = dp // (2 * NZ), lax.rem(dp // 2, NZ), lax.rem(dp, 2)
    zc, zb = lax.rem(z, 4), z // 4

    def device(x, y, z, c):
        return ((x * NZ + z) * 2 + c, y)

    def along_x(d):
        return device(lax.rem(x + d + NX, NX), y, z, c)

    def along_y(d):
        return device(x, lax.rem(y + d + NY, NY), z, c)

    def along_z(d, core=None):
        return device(x, y, lax.rem(z + d + NZ, NZ), c if core is None else core)

    def in_plane(dx, dy, dc):
        return device(lax.rem(x + dx, NX), lax.rem(y + dy, NY), z, lax.rem(c + dc, 2))

    other_core = device(x, y, z, 1 - c)
    sides = [along_x(1), along_x(-1), along_y(1), along_y(-1)]

    def signal(sem, devices):
        for to in devices:
            pl.semaphore_signal(sem, inc=1, device_id=to, device_id_type=MESH)

    barrier = pltpu.get_barrier_semaphore()
    near = [other_core, along_z(1), along_z(-1)] + sides
    signal(barrier, near)
    rounds = [
        sides + [along_z(1), along_z(-1)],
        sides + [along_z(2), along_z(-2)],
        sides + [along_z(4), along_z(-4)],
        [along_z(8), along_z(-8)],
    ]

    def say(n):
        signal(hello.at[n], rounds[n])

    def hear(n):
        pl.semaphore_wait(hello.at[n], len(rounds[n]))

    def columns_of(k):
        return pl.ds(pl.multiple_of(lax.rem(x + k, 4) * 1024, 1024), 1024)

    get_si = pltpu.make_async_copy(si_hbm, si, local_sem.at[0])
    get_og = [
        pltpu.make_async_copy(
            og_hbm.at[:, columns_of(k)], og.at[:, columns_of(k)], local_sem.at[1 + n]
        )
        for n, k in enumerate(ORDER)
    ]
    get_w = pltpu.make_async_copy(w_hbm, w, local_sem.at[5])
    get_hist = pltpu.make_async_copy(hist_hbm, hist_ref, local_sem.at[7])
    get_si.start()
    for copy in get_og:
        copy.start()
    get_hist.start()

    used = [0]
    sent = []

    def send(src, dst, to):
        n = used[0]
        used[0] += 1
        copy = pltpu.make_async_remote_copy(
            src_ref=src, dst_ref=dst, send_sem=send_sem.at[n], recv_sem=recv_sem.at[n],
            device_id=to, device_id_type=MESH,
        )
        copy.start()
        sent.append(copy)
        return copy


    def group(at, i, core):
        return pl.ds(pl.multiple_of(at * 1024 + i * 256 + core * 128, 128), 128)

    get_si.wait()
    si_sent[...] = si[...].astype(F32)
    og_copies = []
    for n, k in enumerate(ORDER):
        get_og[n].wait()
        for i in range(4):
            og_sent[n, :, i * 128 : i * 128 + 128] = og[
                :, group(lax.rem(x + k, 4), i, 1 - c)
            ].astype(F32)
        if n == 0:
            pl.semaphore_wait(barrier, len(near))
            si_copy = send(si_sent, si_core, other_core)
        og_copies.append(send(og_sent.at[n], og_core.at[n], other_core))
    get_w.start()
    say(0)
    get_hist.wait()
    scale_in = LIMIT / jnp.max(hist_ref[...])

    def quantized(grads, inputs):
        term = lax.dot_general(
            grads, inputs, (((0,), (0,)), ((), ())), preferred_element_type=F32
        )
        return jnp.clip(term * scale_in, -LIMIT, LIMIT).astype(BF16).astype(F32)

    def pieces(at, n, first):
        for i in range(2):
            for j in range(4):
                for core in range(2):
                    row = i * 128 + j * 32 + core * 16
                    yield (0, at, j, first + i, core), row
                    yield (1, j, n, first + i, core), row + 8

    def own_tile(n, k):
        at = lax.rem(x + k, 4)

        @pl.loop(0, 2)
        def _(s):
            grads = jnp.concatenate(
                [og[:, group(at, 2 * s, c)], og[:, group(at, 2 * s + 1, c)]], axis=1
            )
            quant = quantized(grads, si[...])
            for where, row in pieces(at, n, 2 * s):
                terms[where] = quant[row : row + 8]

    def other_tile(n, k):
        at = lax.rem(x + k, 4)
        if n == 0:
            si_copy.wait_recv()
            si_other[...] = si_core[...].astype(BF16)
        og_copies[n].wait_recv()

        @pl.loop(0, 2)
        def _(s):
            columns = pl.ds(pl.multiple_of(s * 256, 256), 256)
            quant = quantized(og_core[n, :, columns].astype(BF16), si_other[...])
            for where, row in pieces(at, n, 2 * s):
                terms[where] += quant[row : row + 8]

    A, B = pl.ds(0, 2), pl.ds(2, 2)
    plus = (along_x(1), along_z(1))
    minus = (along_x(-1), along_z(-1))
    first = (x, zc)

    def unit(p, k):
        return terms.at[p, lax.rem(first[p] + k, 4)]

    one = [{}, {}]
    own_tile(0, 2)
    other_tile(0, 2)
    one[0]["a+"] = send(unit(0, 2).at[A], pass_one.at[0, 0], plus[0])
    one[0]["a-"] = send(unit(0, 2).at[B], pass_one.at[0, 1], minus[0])
    hear(0)
    say(1)
    own_tile(1, 1)
    other_tile(1, 1)
    one[1]["a+"] = send(unit(1, 2).at[A], pass_one.at[1, 0], plus[1])
    one[0]["b+"] = send(unit(0, 1).at[B], in_one.at[0, 0, B], plus[0])
    one[1]["b-"] = send(unit(1, 3).at[A], in_one.at[1, 1, A], minus[1])
    own_tile(2, 3)
    other_tile(2, 3)
    one[0]["b-"] = send(unit(0, 3).at[A], in_one.at[0, 1, A], minus[0])
    own_tile(3, 0)
    other_tile(3, 0)
    one[1]["a-"] = send(unit(1, 2).at[B], pass_one.at[1, 1], minus[1])
    one[1]["b+"] = send(unit(1, 1).at[B], in_one.at[1, 0, B], plus[1])
    hear(1)
    say(2)

    def pass_on(p, k, half, at, key_in, key_out, to):
        one[p][key_in].wait_recv()
        m = lax.rem(first[p] + k, 4)
        terms[p, m, half] += pass_one[p, at]
        one[p][key_out] = send(terms.at[p, m, half], in_one.at[p, at, half], to)

    pass_on(0, 1, A, 0, "a+", "c+", plus[0])
    pass_on(0, 3, B, 1, "a-", "c-", minus[0])
    pass_on(1, 1, A, 0, "a+", "c+", plus[1])
    pass_on(1, 3, B, 1, "a-", "c-", minus[1])

    get_w.wait()

    @pl.loop(0, 2)
    def _(i):
        rows = pl.ds(pl.multiple_of(i * 256, 256), 256)
        ig[:, rows] = lax.dot_general(
            og[...], w[rows, :], (((1,), (1,)), ((), ())), preferred_element_type=F32
        ).astype(BF16)

    put_ig = pltpu.make_async_copy(ig, ig_out, local_sem.at[6])
    put_ig.start()
    hear(2)
    say(3)

    C, D = pl.ds(0, 2), pl.ds(2, 2)
    two = [{}, {}]
    up, down = (plus[1], plus[0]), (minus[1], minus[0])

    def second(p, k):
        return lax.rem(zc + k, 4) if p == 0 else PLACE[k]

    def second_start(p):
        for key in ("b+", "b-", "c+", "c-"):
            one[p][key].wait_recv()
        m = first[p]

        def total(k):
            q = second(p, k)
            terms[p, m, q] += in_one[p, 0, q] + in_one[p, 1, q]
            return terms.at[p, m, q]

        far = total(2)
        two[p]["a+"] = send(far.at[C], pass_two.at[p, 0], up[p])
        two[p]["a-"] = send(far.at[D], pass_two.at[p, 1], down[p])
        two[p]["b+"] = send(total(1).at[D], in_two.at[p, 0, D], up[p])
        two[p]["b-"] = send(total(3).at[C], in_two.at[p, 1, C], down[p])
        total(0)

    def second_pass(p):
        m = first[p]
        for key, out, k, half, at, to in (
            ("a+", "c+", 1, C, 0, up[p]),
            ("a-", "c-", 3, D, 1, down[p]),
        ):
            q = second(p, k)
            two[p][key].wait_recv()
            terms[p, m, q, half] += pass_two[p, at]
            two[p][out] = send(terms.at[p, m, q, half], in_two.at[p, at, half], to)

    def second_end(p):
        for key in ("b+", "b-", "c+", "c-"):
            two[p][key].wait_recv()
        ready[:, p] = terms[p, first[p], second(p, 0)] + in_two[p, 0] + in_two[p, 1]

    even = lax.rem(zb, 2) == c
    odd = jnp.logical_not(even)

    def block(k):
        return lax.rem(zb + k, NB) // 2

    def last_copy(n, src, dst, recv, to):
        return pltpu.make_async_remote_copy(
            src_ref=src, dst_ref=dst, send_sem=last_send.at[n], recv_sem=recv,
            device_id=to, device_id_type=MESH,
        )

    def piece(n, k, p, core):
        return last_copy(
            n, ready.at[block(k), p, core], in_last.at[k, p], last_recv.at[2 * k + p],
            along_z(4 * k, core),
        )

    def to_core(n, p):
        return last_copy(
            n, ready.at[block(0), p, 1 - c], in_last.at[0, p], last_recv.at[p], other_core
        )

    def relay_half(n, p, at):
        return last_copy(
            n, ready.at[block(4), p, at], relay_far.at[p, at], relay_sem.at[2 * p + at],
            along_z(8 if at == 0 else -8),
        )

    def relay_whole(n, p, at):
        return last_copy(
            n, ready.at[block(3 if at == 0 else 5), p], relay.at[p, at],
            relay_sem.at[4 + 2 * p + at], along_z(4 if at == 0 else -4),
        )

    def even_first(p):
        return [relay_half(8 * p, p, 0), relay_half(8 * p + 1, p, 1), to_core(8 * p + 2, p)]

    def even_then(p, k):
        n = 8 * p + (3 if k == 2 else 5)
        return [piece(n, k, p, 0), piece(n + 1, k, p, 1)]

    def odd_copies(p):
        n = 8 * p
        return [
            relay_whole(n, p, 0), relay_whole(n + 1, p, 1), piece(n + 2, 1, p, 0),
            piece(n + 3, 7, p, 0), piece(n + 4, 1, p, 1), piece(n + 5, 7, p, 1),
        ]

    def last_start(p):
        @pl.when(even)
        def _():
            for copy in even_first(p):
                copy.start()
            in_last[0, p] = ready[zb // 2, p, c]

        @pl.when(odd)
        def _():
            for copy in odd_copies(p)[:2]:
                copy.start()
            if p == 1:
                for copy in odd_copies(0)[2:] + odd_copies(1)[2:]:
                    copy.start()

    def last_pass(p):
        @pl.when(even)
        def _():
            for at, k in ((0, 2), (1, 6)):
                relay_whole(0, p, at).wait_recv()
                ready[block(k), p] += relay[p, at]
                relay_half(0, p, at).wait_recv()
                ready[block(k), p, at] += relay_far[p, at]
                for copy in even_then(p, k):
                    copy.start()

        @pl.when(odd)
        def _():
            last_copy(
                0, in_last.at[0, p], in_last.at[0, p], last_recv.at[p], other_core
            ).wait_recv()

    second_start(0)
    second_start(1)
    second_pass(0)
    second_pass(1)
    second_end(0)
    hear(3)
    last_start(0)
    second_end(1)
    last_start(1)
    for p in range(2):
        last_pass(p)
    for p in range(2):
        for k in (1, 7, 2, 6):
            piece(0, k, p, 0).wait_recv()
    summed = in_last[0]
    for k in (1, 7, 2, 6):
        summed = summed + in_last[k]
    weight_sum = summed / scale_in

    one_row = pl.ds(0, 1)

    def largest(best, at, slots, devices):
        peak[at, 0:1, :] = best
        copies = [
            (d, send(peak.at[at, one_row], slots.at[d, one_row], to)) for d, to in devices
        ]
        for d, copy in copies:
            copy.wait_recv()
            best = jnp.maximum(best, slots[d, 0:1, :])
        return best

    def way(d, n):
        return min(d, n - d)

    plane = sorted(
        range(2, 2 * NX * NY, 2), key=lambda d: -way(d // 2 // NY, NX) - way(d // 2 % NY, NY)
    )
    line = sorted(range(1, NZ), key=lambda d: -way(d, NZ))
    top = jnp.max(jnp.max(jnp.abs(weight_sum), axis=0), axis=0, keepdims=True)
    best = top[:, 0:128]
    for i in range(1, 4):
        best = jnp.maximum(best, top[:, i * 128 : i * 128 + 128])
    best = largest(
        best, 0, peaks_plane, [(d, in_plane(d // 2 // NY, d // 2 % NY, d % 2)) for d in plane]
    )
    best = largest(best, 1, peaks_z, [(d, along_z(d)) for d in line])
    best = largest(best, 2, peaks_plane, [(1, other_core)])
    amax = jnp.max(best, axis=1, keepdims=True)

    lane = lax.broadcasted_iota(jnp.int32, (1, 16), 1)
    new_history = jnp.where(lane == 0, amax, jnp.roll(hist_ref[...], 1, axis=1))
    hist_out[...] = new_history
    out_scale = LIMIT / jnp.max(new_history)
    wq_out[...] = (weight_sum * out_scale).reshape(16, 512)

    for copy in sent:
        copy.wait_send()

    @pl.when(even)
    def _():
        for p in range(2):
            for copy in even_first(p) + even_then(p, 2) + even_then(p, 6):
                copy.wait_send()

    @pl.when(odd)
    def _():
        for p in range(2):
            for copy in odd_copies(p):
                copy.wait_send()

    put_ig.wait()


def write_out(ig_in, wq_in, hist_in, ig_out, wq_out, hist_out):
    ig_out[...] = ig_in[...]
    wq_out[...] = wq_in[...].astype(BF16)
    hist_out[...] = hist_in[...]


def shards(out_grad, saved_input, weight, amax_history):
    any_space = pl.BlockSpec(memory_space=pl.ANY)
    vmem = pl.BlockSpec(memory_space=pltpu.VMEM)
    part = (8, 512)
    input_grad, weight_q, history = pl.pallas_call(
        kernel,
        out_shape=(
            jax.ShapeDtypeStruct((192, 512), BF16),
            jax.ShapeDtypeStruct((16, 512), F32),
            jax.ShapeDtypeStruct((1, 16), F32),
        ),
        in_specs=[any_space] * 4,
        out_specs=[any_space, vmem, vmem],
        scratch_shapes=[
            pltpu.VMEM((1, 16), F32),
            pltpu.VMEM((192, 4096), BF16),
            pltpu.VMEM((192, 512), BF16),
            pltpu.VMEM((512, 4096), BF16),
            pltpu.VMEM((192, 512), BF16),
            pltpu.VMEM((192, 512), F32),
            pltpu.VMEM((4, 192, 512), F32),
            pltpu.VMEM((192, 512), F32),
            pltpu.VMEM((4, 192, 512), F32),
            pltpu.VMEM((192, 512), BF16),
            pltpu.VMEM((2, 4, 4, 4, 2) + part, F32),
            pltpu.VMEM((2, 2, 2, 4, 2) + part, F32),
            pltpu.VMEM((2, 2, 4, 4, 2) + part, F32),
            pltpu.VMEM((2, 2, 2, 2) + part, F32),
            pltpu.VMEM((2, 2, 4, 2) + part, F32),
            pltpu.VMEM((4, 2, 2) + part, F32),
            pltpu.VMEM((2, 2, 2) + part, F32),
            pltpu.VMEM((2, 2) + part, F32),
            pltpu.VMEM((NB, 2) + part, F32),
            pltpu.VMEM((2 * NX * NY, 8, 128), F32),
            pltpu.VMEM((NZ, 8, 128), F32),
            pltpu.VMEM((3, 8, 128), F32),
            pltpu.SemaphoreType.DMA((8,)),
            pltpu.SemaphoreType.DMA((N_SENT,)),
            pltpu.SemaphoreType.DMA((N_SENT,)),
            pltpu.SemaphoreType.DMA((16,)),
            pltpu.SemaphoreType.DMA((2 * NB,)),
            pltpu.SemaphoreType.DMA((8,)),
            pltpu.SemaphoreType.REGULAR((4,)),
        ],
        compiler_params=pltpu.CompilerParams(
            collective_id=0, has_side_effects=True, vmem_limit_bytes=60 * 2**20
        ),
        name="all_steps",
    )(out_grad, saved_input, weight, amax_history.reshape(1, 16))
    input_grad, weight_q, history = pl.pallas_call(
        write_out,
        out_shape=(
            jax.ShapeDtypeStruct((192, 512), BF16),
            jax.ShapeDtypeStruct((16, 512), BF16),
            jax.ShapeDtypeStruct((1, 16), F32),
        ),
        in_specs=[vmem, vmem, vmem],
        out_specs=[vmem, vmem, vmem],
        compiler_params=pltpu.CompilerParams(vmem_limit_bytes=60 * 2**20),
        name="write_out",
    )(input_grad, weight_q, history)
    return (input_grad, weight_q.T, history.reshape(16))


def solution(mesh):
    placed = (P("dp", None), P("dp", "tensor"), P("tensor", None), P())
    return jax.shard_map(
        shards,
        mesh=mesh,
        in_specs=placed,
        out_specs=(P("dp", "tensor"), P("tensor", "dp"), P()),
        check_vma=False,
    )
```
